32 devices in a mesh: dp: 16 (over z, x, core), rep: 2 (over y).
Axes of the slice: x: 2, y: 2, z: 4, core: 2. Of those that a mesh axis runs over, the one named last changes fastest.
Arguments:
- text_states: bfloat16 [14336, 1280], P(('dp', 'rep')), may hold values from -6 to 6
- encoder_frames: bfloat16 [16384, 1280], P(('dp', 'rep')), may hold values from -20 to 20
- out_cotangent: bfloat16 [14336, 1280], P(('dp', 'rep')), may hold values from -6 to 6
- text_lengths: int32 [32], P(('dp', 'rep')), may hold values from 1 to 448, 10752 in all
- q_master: float32 [1280, 640], P('dp'), may hold values from -0.15625 to 0.15625
- q_moment: float32 [1280, 640], P('dp'), may hold values from -3 to 3
- q_second: float32 [1280, 640], P('dp'), may hold values from 0.05 to 2
- key_weight: bfloat16 [1280, 640], P('dp'), may hold values from -0.15625 to 0.15625
- value_weight: bfloat16 [1280, 640], P('dp'), may hold values from -0.15625 to 0.15625
- out_weight: bfloat16 [640, 1280], P(None, 'dp'), may hold values from -0.25 to 0.25
Outputs:
- block_out: bfloat16 [14336, 1280], P(('dp', 'rep'))
- q_gradient: float32 [1280, 640], P('dp')
- new_master: float32 [1280, 640], P('dp')
- new_moment: float32 [1280, 640], P('dp')
- new_second: float32 [1280, 640], P('dp')
The draws below stay inside these ranges and needn't reach their ends.
All inputs are finite; a program needn't handle non-finite values. No bound on the sum of `text_lengths` on one device may be relied on, other than what follows from the above.
Results may differ from the reference program's by a relative error of at most 0.017.
The reference program's roundings to bfloat16 on the way (of `q_weight`, `queries`, `attention`, `context`, `grad_out`, `grad_context`, `grad_scores` and `grad_queries`) count: a program that leaves them out, or rounds other values in their place, can miss the bound.
Values may be sent and summed in bfloat16 or wider, within the bound.
No kernel may reach another device: no remote copies, remote signals or barrier semaphores. Data moves between devices by JAX's collectives and lax.ppermute only.
A program may use at most 64 MiB of HBM per device.

```python
import math
import jax
import jax.numpy as jnp
import numpy as np
from jax import lax

D = 1280
HEADS = 10
HEAD_DIM = 64
TOK = 448
FRAMES = 512
HD = 640
CLIPS = 32


def draw_encoder_frames(key, part):
    key = jax.random.fold_in(key, 7)
    base_key = jax.random.fold_in(key, 0)
    frames = jnp.clip(jax.random.normal(base_key, (CLIPS * FRAMES, D), jnp.float32), -6.0, 6.0)
    return frames.astype(jnp.bfloat16)


def steps_of(own_key, dims, shards, least, largest):
    level = 1.0
    for axis_at, blocks in shards:
        steps = jax.random.uniform(jax.random.fold_in(jax.random.fold_in(own_key, 6), axis_at), (blocks,), jnp.float32, least / len(shards), largest / len(shards))
        level = level * jnp.repeat(jnp.exp(steps), dims[axis_at] // blocks).reshape((-1,) + (1,) * (len(dims) - 1 - axis_at))
    return level


def split_up(number_of, total, most, skew):
    loads = [(1 << 20) // math.isqrt(grade ** skew) + 1 for grade in range(2, number_of + 1)]
    surplus, given = total - most - (number_of - 1), [1] * (number_of - 1)
    while surplus > 0:
        candidates = [i for i in range(number_of - 1) if given[i] < most]
        whole, left = sum([loads[i] for i in candidates]), surplus
        for i in candidates:
            addition = min(most - given[i], max(1, left * loads[i] // whole), surplus)
            given[i] = given[i] + addition
            surplus = surplus - addition
    return np.array([most] + given)


def ragged_sizes(own_key, count, total, most, lean):
    if count == 2:
        one = jax.random.randint(own_key, (), max(1, total - most), min(most, total - 1) + 1)
        return jnp.stack([one, total - one])
    lengths = jnp.asarray(split_up(count, total, most, lean), jnp.int32)
    twos = (count - 1) // 2
    donor, sink = lengths[1:1 + 2 * twos:2], lengths[2:2 + 2 * twos:2]
    margin = jnp.minimum(donor - 1, most - sink)
    passed = jax.random.randint(jax.random.fold_in(own_key, 1), (twos,), 0, 1 << 20) % (margin + 1)
    lengths = lengths.at[1:1 + 2 * twos:2].set(donor - passed).at[2:2 + 2 * twos:2].set(sink + passed)
    return lengths[jax.random.permutation(jax.random.fold_in(own_key, 2), count)]


def centred(stream_key, extent, width, bound, cuts=(), kind=jnp.bfloat16):
    level = steps_of(stream_key, extent, cuts, -0.22, 0.18) if cuts else 1.0
    values = jax.random.normal(stream_key, extent, jnp.float32) * width * level
    return jnp.minimum(jnp.maximum(values, -bound), bound).astype(kind)


def setup_inputs(seed: int = 0) -> dict:
    arg_keys = jax.random.split(jax.random.key(seed), 11)
    text_states = centred(arg_keys[0], (CLIPS * TOK, D), 1.0, 6.0, ((0, 32),))
    encoder_frames = draw_encoder_frames(jax.random.fold_in(arg_keys[10], 71), 0)
    out_cotangent = centred(arg_keys[2], (CLIPS * TOK, D), 1.0, 6.0, ((0, 32),))
    text_lengths = ragged_sizes(arg_keys[3], CLIPS, CLIPS * (3 * TOK // 4), TOK, 0).astype(jnp.int32)
    q_master = centred(arg_keys[4], (D, HD), D ** -0.5, 0.15625, ((0, 16),), jnp.float32)
    q_moment = centred(arg_keys[5], (D, HD), 0.5, 3.0, ((0, 16),), jnp.float32)
    q_second = jnp.clip(jnp.exp(math.log(2.0) - 3.6888794 * jax.random.uniform(arg_keys[6], (D, HD), jnp.float32) ** steps_of(arg_keys[6], (D, HD), ((0, 16),), -0.2, 0.2)), 0.05, 2.0)
    key_weight = centred(arg_keys[7], (D, HD), D ** -0.5, 0.15625, ((0, 16),))
    value_weight = centred(arg_keys[8], (D, HD), D ** -0.5, 0.15625, ((0, 16),))
    out_weight = centred(arg_keys[9], (HD, D), HD ** -0.5, 0.25, ((1, 16),))
    return {"text_states": text_states, "encoder_frames": encoder_frames, "out_cotangent": out_cotangent, "text_lengths": text_lengths, "q_master": q_master, "q_moment": q_moment, "q_second": q_second, "key_weight": key_weight, "value_weight": value_weight, "out_weight": out_weight}


first_fix = 0.9999734386011124
second_fix = 0.8673804441052468

def one_clip(text_rows, frame_rows, cot_rows, length, q_weight, key_weight, value_weight, out_weight):
    scale = HEAD_DIM ** (-0.5)
    queries = jnp.dot(text_rows, q_weight, preferred_element_type=jnp.float32).astype(jnp.bfloat16)
    keys_all = jnp.dot(frame_rows, key_weight, preferred_element_type=jnp.float32).astype(jnp.bfloat16)
    values_all = jnp.dot(frame_rows, value_weight, preferred_element_type=jnp.float32).astype(jnp.bfloat16)
    query_heads = queries.reshape(TOK, HEADS, HEAD_DIM).astype(jnp.float32)
    key_heads = keys_all.reshape(FRAMES, HEADS, HEAD_DIM).astype(jnp.float32)
    value_heads = values_all.reshape(FRAMES, HEADS, HEAD_DIM).astype(jnp.float32)
    scores = jnp.einsum('thd,fhd->htf', query_heads, key_heads) * scale
    attention = jax.nn.softmax(scores, axis=-1).astype(jnp.bfloat16)
    attn_float = attention.astype(jnp.float32)
    context = jnp.einsum('htf,fhd->thd', attn_float, value_heads).reshape(TOK, HD).astype(jnp.bfloat16)
    block_rows = jnp.dot(context, out_weight, preferred_element_type=jnp.float32).astype(jnp.bfloat16)
    in_use = jnp.arange(TOK, dtype=jnp.int32) < length
    grad_out = jnp.where(in_use[:, None], cot_rows, jnp.zeros_like(cot_rows))
    grad_context = jnp.dot(grad_out, out_weight.T, preferred_element_type=jnp.float32).astype(jnp.bfloat16)
    grad_heads = grad_context.reshape(TOK, HEADS, HEAD_DIM).astype(jnp.float32)
    grad_attention = jnp.einsum('thd,fhd->htf', grad_heads, value_heads)
    inner = lax.optimization_barrier(jnp.sum(attn_float * grad_attention, axis=-1, keepdims=True))
    grad_scores = (attn_float * (grad_attention - inner) * scale).astype(jnp.bfloat16)
    grad_queries = jnp.einsum('htf,fhd->thd', grad_scores.astype(jnp.float32), key_heads).reshape(TOK, HD).astype(jnp.bfloat16)
    partial_grad = jnp.dot(text_rows.T, grad_queries, preferred_element_type=jnp.float32)
    return (block_rows, partial_grad)

def reference(text_states, encoder_frames, out_cotangent, text_lengths, q_master, q_moment, q_second, key_weight, value_weight, out_weight):
    q_weight = q_master.astype(jnp.bfloat16)
    text_clips = text_states.reshape(CLIPS, TOK, D)
    frame_clips = encoder_frames.reshape(CLIPS, FRAMES, D)
    cot_clips = out_cotangent.reshape(CLIPS, TOK, D)

    def step_fn(carry, inputs):
        text_rows, frame_rows, cot_rows, length = inputs
        block_rows, partial_grad = one_clip(text_rows, frame_rows, cot_rows, length, q_weight, key_weight, value_weight, out_weight)
        return (carry + partial_grad, block_rows)
    summed, block_all = lax.scan(step_fn, jnp.zeros((D, HD), jnp.float32), (text_clips, frame_clips, cot_clips, text_lengths.astype(jnp.int32)))
    q_gradient = summed * (1.0 / TOK)
    new_moment = 0.9 * q_moment + 0.1 * q_gradient
    new_second = 0.98 * q_second + 0.02 * q_gradient * q_gradient
    update = new_moment / first_fix / (jnp.sqrt(new_second / second_fix) + 1e-06)
    new_master = q_master - 0.001 * (update + 0.01 * q_master)
    return (block_all.reshape(CLIPS * TOK, D), q_gradient, new_master, new_moment, new_second)
```

```python
import functools

import jax
import jax.numpy as jnp
from jax import lax
from jax.experimental import pallas as pl
from jax.experimental.pallas import tpu as pltpu
from jax.sharding import PartitionSpec as P

HEADS = 10
HEAD_DIM = 64
TOK = 448
CORES = 2
CORE_HEADS = HEADS // CORES
GROUPS = ((0, 3), (3, 2))
RING_MOST = 8

first_fix = 0.9999734386011124
second_fix = 0.8673804441052468
BF = jnp.bfloat16
F32 = jnp.float32


def dot(a, b, dims=((1,), (0,))):
    return lax.dot_general(a, b, (dims, ((), ())), preferred_element_type=F32)


def ring_order(chips):
    return list(range(0, chips, 2)) + list(range(chips - 1, 0, -2))


def ring_pairs(chips, step):
    order = ring_order(chips)
    return [
        (CORES * order[i] + c, CORES * order[(i + step) % chips] + c)
        for i in range(chips)
        for c in range(CORES)
    ]


def head_kernel(number, rows_of, pieces, *refs):
    width = number * HEAD_DIM
    refs = list(refs)
    take = lambda n: [refs.pop(0) for _ in range(n)]
    (offs,) = take(1)
    blocks = take(len(rows_of))
    acts = take(8)
    (share, ctx_own) = take(2)
    sums = take(len(pieces))
    (w, x0, x1, e0, e1, g0, g1, t0, t1, wsem, asem) = take(11)
    acts_v = (x0, x1, e0, e1, g0, g1, t0, t1)
    copies = [
        pltpu.make_async_copy(
            b, w.at[pl.ds(pl.multiple_of(offs[i], 16 if n % 16 == 0 else n), n)], wsem.at[i]
        )
        for i, (b, n) in enumerate(zip(blocks, rows_of))
    ]
    loads = [pltpu.make_async_copy(a, v, asem.at[i]) for i, (a, v) in enumerate(zip(acts, acts_v))]
    for c in copies + loads:
        c.start()
    for c in copies:
        c.wait()
    wq, wk, wv, wo = [w[:, i * width : (i + 1) * width] for i in range(4)]
    grads = []
    for clip in range(2):
        xs, es, gs_ = acts_v[clip], acts_v[2 + clip], acts_v[4 + clip]
        loads[clip].wait()
        q = (dot(xs[...], wq) * 0.125).astype(BF)
        loads[2 + clip].wait()
        k = dot(es[...], wk).astype(BF)
        v = dot(es[...], wv).astype(BF)
        loads[4 + clip].wait()
        gc = dot(gs_[...], wo).astype(BF)
        ctxs, gqs = [], []
        for h in range(number):
            cols = slice(h * HEAD_DIM, (h + 1) * HEAD_DIM)
            qh, kh, vh, gh = q[:, cols], k[:, cols], v[:, cols], gc[:, cols]
            s = dot(qh, kh, ((1,), (1,)))
            p = jnp.exp(s - jnp.max(s, axis=1, keepdims=True))
            a = (p * (1.0 / jnp.sum(p, axis=1, keepdims=True))).astype(BF)
            ctx = dot(a, vh)
            ga = dot(gh, vh, ((1,), (1,)))
            inner = jnp.sum(gh.astype(F32) * ctx, axis=1, keepdims=True)
            gs = (a.astype(F32) * (ga - inner)).astype(BF)
            gqs.append((dot(gs, kh) * 0.125).astype(BF))
            ctxs.append(ctx.astype(BF))
        grads.append(jnp.concatenate(gqs, axis=1))
        if clip == 0:
            ctx_own[...] = jnp.concatenate(ctxs, axis=1)
        else:
            share[:TOK, :] = jnp.concatenate(ctxs, axis=1)
    share[TOK:, :] = wo
    loads[6].wait()
    loads[7].wait()
    for out, (at, skip, n) in zip(sums, pieces):
        rows = pl.ds(pl.multiple_of(offs[at], 16 if n % 16 == 0 else n) + skip, n)
        out[...] = dot(t0[rows, :], grads[0]) + dot(t1[rows, :], grads[1])


def head_group(number, offs, blocks, rows_of, pieces, acts):
    depth = acts[6].shape[0]
    frames = acts[2].shape[0]
    width = number * HEAD_DIM
    hbm = pl.BlockSpec(memory_space=pl.ANY)
    vm = pl.BlockSpec(memory_space=pltpu.VMEM)
    return pl.pallas_call(
        functools.partial(head_kernel, number, rows_of, pieces),
        out_shape=(
            jax.ShapeDtypeStruct((TOK + depth, width), BF),
            jax.ShapeDtypeStruct((TOK, width), BF),
        )
        + tuple(jax.ShapeDtypeStruct((n, width), F32) for _, _, n in pieces),
        in_specs=[pl.BlockSpec(memory_space=pltpu.SMEM)] + [hbm] * (len(blocks) + 8),
        out_specs=(vm,) * (2 + len(pieces)),
        scratch_shapes=[
            pltpu.VMEM((depth, 4 * width), BF),
            pltpu.VMEM((TOK, depth), BF),
            pltpu.VMEM((TOK, depth), BF),
            pltpu.VMEM((frames, depth), BF),
            pltpu.VMEM((frames, depth), BF),
            pltpu.VMEM((TOK, depth), BF),
            pltpu.VMEM((TOK, depth), BF),
            pltpu.VMEM((depth, TOK), BF),
            pltpu.VMEM((depth, TOK), BF),
            pltpu.SemaphoreType.DMA((len(blocks),)),
            pltpu.SemaphoreType.DMA((8,)),
        ],
        compiler_params=pltpu.CompilerParams(vmem_limit_bytes=48 * 2**20),
        cost_estimate=pl.CostEstimate(
            flops=number * 2 * 2 * 480 * 64 * (5 * depth + 4 * 512),
            bytes_accessed=2 * 4 * 1280 * 960 * 2,
            transcendentals=number * 2 * TOK * frames,
        ),
    )(offs, *blocks, *acts)


def per_device(
    chips,
    reps,
    text_states,
    encoder_frames,
    out_cotangent,
    text_lengths,
    q_master,
    q_moment,
    q_second,
    key_weight,
    value_weight,
    out_weight,
):
    rows, width = q_master.shape
    depth = text_states.shape[1]
    half = width // CORES
    me = lax.axis_index("dp")
    core, chip = me % CORES, me // CORES
    first = core == 0
    mates = [(i, i ^ 1) for i in range(CORES * chips)]
    swap = lambda a: lax.ppermute(a, "dp", mates)
    ring = 1 < chips <= RING_MOST
    right = lambda a: lax.ppermute(a, "dp", ring_pairs(chips, 1))
    left = lambda a: lax.ppermute(a, "dp", ring_pairs(chips, -1))

    parts = (q_master.astype(BF), key_weight, value_weight, out_weight.T)
    def pack(c):
        return jnp.concatenate(
            [
                w[:, c * half + h * HEAD_DIM : c * half + (h + n) * HEAD_DIM]
                for h, n in GROUPS
                for w in parts
            ],
            axis=1,
        )
    packs = [pack(c) for c in range(CORES)]
    keep = jnp.where(first, packs[0], packs[1])
    got = swap(jnp.where(first, packs[1], packs[0]))
    block = jnp.where(
        first, jnp.concatenate([keep, got], axis=0), jnp.concatenate([got, keep], axis=0)
    )

    in_use = jnp.arange(TOK, dtype=jnp.int32) < text_lengths[0]
    grad_out = jnp.where(in_use[:, None], out_cotangent, jnp.zeros_like(out_cotangent))
    x0, e0, g0 = text_states, encoder_frames, grad_out
    x1, e1, g1 = swap(x0), swap(e0), swap(g0)
    acts = (x0, x1, e0, e1, g0, g1, x0.T, x1.T)

    chip_rows = CORES * rows
    lower = chip_rows // 2
    if ring:
        order = ring_order(chips)
        place = [order.index(c) for c in range(chips)]
        table = [
            [chip_rows * order[(place[c] + k) % chips] for k in range(chips)] for c in range(chips)
        ]
        at = jnp.asarray(table, jnp.int32)[chip]
        far = chips // 2
    starts = [4 * HEAD_DIM * h for h, _ in GROUPS]
    shares, owns, totals = [], [], []
    for (h, n), start in zip(GROUPS, starts):
        mine = block[:, start : start + 4 * HEAD_DIM * n]
        if ring:
            blocks, steps = [mine], [0]
            r = l = mine
            for k in range(1, far):
                r, l = right(r), left(l)
                blocks += [r, l]
                steps += [chips - k, k]
            blocks += [right(r[:lower]), left(l[lower:])]
            offs = jnp.stack([at[k] for k in steps] + [at[far], at[far] + lower])
            rows_of = [chip_rows] * len(steps) + [lower, lower]
            pieces = [(len(steps), 0, lower), (len(steps), lower, lower)]
            for k in range(far - 1, 0, -1):
                pieces += [(steps.index(k), 0, chip_rows), (steps.index(chips - k), 0, chip_rows)]
            pieces += [(0, 0, chip_rows)]
            pieces[1] = (len(steps) + 1, 0, lower)
        else:
            blocks = [
                lax.all_gather(
                    mine,
                    "dp",
                    axis=0,
                    tiled=True,
                    axis_index_groups=[
                        [CORES * i + c for i in range(chips)] for c in range(CORES)
                    ],
                )
            ]
            offs = jnp.zeros((1,), jnp.int32)
            rows_of = [depth]
            pieces = [(0, 0, depth)]
        share, own, *sums = head_group(n, offs, blocks, rows_of, pieces, acts)
        shares.append(share)
        owns.append(own)
        if ring:
            r, l = right(sums[0]), left(sums[1])
            for k in range(far - 1, 0, -1):
                toward_right, toward_left = sums[2 * (far - k)], sums[2 * (far - k) + 1]
                if k == far - 1:
                    r = jnp.concatenate([toward_right[:lower] + r, toward_right[lower:]], axis=0)
                    l = jnp.concatenate([toward_left[:lower], toward_left[lower:] + l], axis=0)
                else:
                    r, l = toward_right + r, toward_left + l
                r, l = right(r), left(l)
            totals.append(sums[-1] + r + l)
        else:
            totals.append(
                lax.psum_scatter(
                    sums[0],
                    "dp",
                    scatter_dimension=0,
                    tiled=True,
                    axis_index_groups=[
                        [CORES * i + c for i in range(chips)] for c in range(CORES)
                    ],
                )
            )

    mine = jnp.concatenate([s[TOK:] for s in shares], axis=1)
    swapped = [swap(s) for s in shares]
    context = jnp.concatenate(owns + [s[:TOK] for s in swapped], axis=1)
    out_rows = jnp.concatenate([s[TOK:] for s in shares + swapped], axis=1)
    block_out = dot(context, out_rows, ((1,), (1,))).astype(BF)

    total = jnp.concatenate(totals, axis=1)
    keep = jnp.where(first, total[:rows], total[rows:])
    got = swap(jnp.where(first, total[rows:], total[:rows]))
    summed = jnp.where(
        first, jnp.concatenate([keep, got], axis=1), jnp.concatenate([got, keep], axis=1)
    )
    if reps == 2:
        summed = summed + lax.ppermute(summed, "rep", [(0, 1), (1, 0)])
    else:
        summed = lax.psum(summed, "rep")
    q_gradient = summed * (1.0 / TOK)
    new_moment = 0.9 * q_moment + 0.1 * q_gradient
    new_second = 0.98 * q_second + 0.02 * q_gradient * q_gradient
    update = new_moment / first_fix / (jnp.sqrt(new_second / second_fix) + 1e-06)
    new_master = q_master - 0.001 * (update + 0.01 * q_master)
    return (block_out, q_gradient, new_master, new_moment, new_second)


def solution(mesh):
    in_specs = (
        P(("dp", "rep"), None),
        P(("dp", "rep"), None),
        P(("dp", "rep"), None),
        P(("dp", "rep")),
        P("dp", None),
        P("dp", None),
        P("dp", None),
        P("dp", None),
        P("dp", None),
        P(None, "dp"),
    )
    out_specs = (P(("dp", "rep"), None), P("dp", None), P("dp", None), P("dp", None), P("dp", None))
    return jax.shard_map(
        functools.partial(per_device, mesh.shape["dp"] // CORES, mesh.shape["rep"]),
        mesh=mesh,
        in_specs=in_specs,
        out_specs=out_specs,
        check_vma=False,
    )
```

```python
import functools

import jax
import jax.numpy as jnp
from jax import lax
from jax.experimental import pallas as pl
from jax.experimental.pallas import tpu as pltpu
from jax.sharding import PartitionSpec as P

HEADS = 10
HEAD_DIM = 64
TOK = 448
CORES = 2
CORE_HEADS = HEADS // CORES
WIDE = CORE_HEADS * HEAD_DIM
ROOM = 384
RING_MOST = 8

first_fix = 0.9999734386011124
second_fix = 0.8673804441052468
BF = jnp.bfloat16
F32 = jnp.float32
VM = pl.BlockSpec(memory_space=pltpu.VMEM)
SM = pl.BlockSpec(memory_space=pltpu.SMEM)
ANY = pl.BlockSpec(memory_space=pl.ANY)
HBM = pl.BlockSpec(memory_space=pltpu.HBM)
SMALL = pltpu.CompilerParams(vmem_limit_bytes=4 * 2**20)


def dot(a, b, dims=((1,), (0,))):
    return lax.dot_general(a, b, (dims, ((), ())), preferred_element_type=F32)


def ring_order(chips):
    return list(range(0, chips, 2)) + list(range(chips - 1, 0, -2))


def ring_pairs(chips, step):
    order = ring_order(chips)
    return [
        (CORES * order[i] + c, CORES * order[(i + step) % chips] + c)
        for i in range(chips)
        for c in range(CORES)
    ]


def chip_at(me_ref, chips, step):
    chip = me_ref[0] // CORES
    odd = chip % 2
    place = (1 - odd) * (chip // 2) + odd * (chips - 1 - chip // 2)
    place = (place + step + chips) % chips
    back = (place >= chips // 2).astype(jnp.int32)
    return (1 - back) * (2 * place) + back * (2 * (chips - 1 - place) + 1)


def pack_kernel(me, q, k, v, o, keep, send, qv, kv, vv, ov, sem):
    copies = [
        pltpu.make_async_copy(src, dst, sem.at[i])
        for i, (src, dst) in enumerate(((q, qv), (k, kv), (v, vv), (o, ov)))
    ]
    for c in copies:
        c.start()
    for c in copies:
        c.wait()
    first = me[0] % CORES == 0
    parts = (qv[...].astype(BF), kv[...], vv[...], ov[...])
    halves = [jnp.concatenate([w[:, c * WIDE : (c + 1) * WIDE] for w in parts], axis=1) for c in (0, 1)]

    @pl.when(first)
    def _():
        keep[...] = halves[0]
        send[...] = halves[1]

    @pl.when(jnp.logical_not(first))
    def _():
        keep[...] = halves[1]
        send[...] = halves[0]


def turn_kernel(x, t):
    t[...] = x[...].T


def turn(x):
    return pl.pallas_call(
        turn_kernel,
        out_shape=jax.ShapeDtypeStruct(x.shape[::-1], BF),
        in_specs=[VM],
        out_specs=VM,
        compiler_params=pltpu.CompilerParams(vmem_limit_bytes=8 * 2**20),
        cost_estimate=pl.CostEstimate(flops=0, bytes_accessed=5 * 10**6, transcendentals=0),
    )(x)


def join_kernel(me, keep, got, *blocks):
    core = me[0] % CORES
    rows = keep.shape[0]
    cols = keep.shape[1] // len(blocks)
    mine = pl.ds(pl.multiple_of(core * rows, rows), rows)
    other = pl.ds(pl.multiple_of((1 - core) * rows, rows), rows)
    for i, block in enumerate(blocks):
        block[mine, :] = keep[:, i * cols : (i + 1) * cols]
        block[other, :] = got[:, i * cols : (i + 1) * cols]


def head_kernel(chips, steps, pieces, *refs):
    refs = list(refs)
    take = lambda n: [refs.pop(0) for _ in range(n)]
    (me,) = take(1)
    blocks = take(2 * len(steps))
    x0, x1, e0, e1, g0, g1, t0, t1 = take(8)
    share, ctx_own = take(2)
    sums = take(len(pieces))
    wqk, wvo, sem = take(3)
    chip_rows = wqk.shape[0] // chips
    if len(steps) == 1:
        places = [0]
    else:
        places = [pl.multiple_of(chip_at(me, chips, k) * chip_rows, chip_rows) for k in range(chips)]
    copies = []
    for i, k in enumerate(steps):
        for j, w in enumerate((wqk, wvo)):
            b = blocks[2 * i + j]
            at = pl.ds(places[k], b.shape[0])
            copies.append(pltpu.make_async_copy(b, w.at[at, :], sem.at[2 * i + j]))
    for c in copies:
        c.start()
    for c in copies:
        c.wait()
    grads = []
    for xs, es, gs in ((x0, e0, g0), (x1, e1, g1)):
        q = (dot(xs[...], wqk[:, :WIDE]) * 0.125).astype(BF)
        k = dot(es[...], wqk[:, WIDE:]).astype(BF)
        v = dot(es[...], wvo[:, :WIDE]).astype(BF)
        gc = dot(gs[...], wvo[:, WIDE:]).astype(BF)
        ctxs, gqs = [], []
        for h in range(CORE_HEADS):
            cols = slice(h * HEAD_DIM, (h + 1) * HEAD_DIM)
            qh, kh, vh, gh = q[:, cols], k[:, cols], v[:, cols], gc[:, cols]
            s = dot(qh, kh, ((1,), (1,)))
            p = jnp.exp(s - jnp.max(s, axis=1, keepdims=True))
            a = (p * (1.0 / jnp.sum(p, axis=1, keepdims=True))).astype(BF)
            ctx = dot(a, vh)
            ga = dot(gh, vh, ((1,), (1,)))
            inner = jnp.sum(gh.astype(F32) * ctx, axis=1, keepdims=True)
            gsc = (a.astype(F32) * (ga - inner)).astype(BF)
            gqs.append((dot(gsc, kh) * 0.125).astype(BF))
            ctxs.append(ctx.astype(BF))
        grads.append(jnp.concatenate(gqs, axis=1))
        if xs is x0:
            ctx_own[...] = jnp.concatenate(ctxs, axis=1)
        else:
            share[:TOK, :WIDE] = jnp.concatenate(ctxs, axis=1)
    share[TOK:, :WIDE] = wvo[:, WIDE:]
    for out, (k, skip) in zip(sums, pieces):
        rows = pl.ds(places[k] + skip, out.shape[0])
        out[...] = dot(t0[rows, :], grads[0]) + dot(t1[rows, :], grads[1])


def heads(chips, me, blocks, steps, acts, pieces, piece_rows):
    depth = acts[6].shape[0]
    return pl.pallas_call(
        functools.partial(head_kernel, chips, steps, pieces),
        out_shape=(
            jax.ShapeDtypeStruct((TOK + depth, ROOM), BF),
            jax.ShapeDtypeStruct((TOK, WIDE), BF),
        )
        + (jax.ShapeDtypeStruct((piece_rows, WIDE), F32),) * len(pieces),
        in_specs=[SM] + [ANY] * len(blocks) + [VM] * 8,
        out_specs=(VM,) * (2 + len(pieces)),
        scratch_shapes=[
            pltpu.VMEM((depth, 2 * WIDE), BF),
            pltpu.VMEM((depth, 2 * WIDE), BF),
            pltpu.SemaphoreType.DMA((len(blocks),)),
        ],
        compiler_params=pltpu.CompilerParams(vmem_limit_bytes=14 * 2**20),
        cost_estimate=pl.CostEstimate(
            flops=9 * 10**9, bytes_accessed=20 * 10**6, transcendentals=2 * 10**6
        ),
    )(me, *blocks, *acts)


def out_kernel(ctx_own, share, got, out):
    out[...] = (
        dot(ctx_own[...], share[TOK:, :WIDE], ((1,), (1,)))
        + dot(got[:TOK, :WIDE], got[TOK:, :WIDE], ((1,), (1,)))
    ).astype(BF)


def total_kernel(me, own0, r0, l0, own1, r1, l1, keep, send):
    first = me[0] % CORES == 0
    low = own0[...] + r0[...] + l0[...]
    high = own1[...] + r1[...] + l1[...]

    @pl.when(first)
    def _():
        keep[...] = low
        send[...] = high

    @pl.when(jnp.logical_not(first))
    def _():
        keep[...] = high
        send[...] = low


def adam(q_master, q_moment, q_second, summed):
    q_gradient = summed * (1.0 / TOK)
    new_moment = 0.9 * q_moment + 0.1 * q_gradient
    new_second = 0.98 * q_second + 0.02 * q_gradient * q_gradient
    update = new_moment / first_fix / (jnp.sqrt(new_second / second_fix) + 1e-06)
    new_master = q_master - 0.001 * (update + 0.01 * q_master)
    return q_gradient, new_master, new_moment, new_second


def step_kernel(me, keep, keep_y, got, got_y, master, moment, second, *outs):
    core = me[0] % CORES
    mine = keep[...] + keep_y[...]
    other = got[...] + got_y[...]
    for c in range(CORES):

        @pl.when(core == c)
        def _():
            summed = jnp.concatenate([mine, other] if c == 0 else [other, mine], axis=1)
            for out, value in zip(outs, adam(master[...], moment[...], second[...], summed)):
                out[...] = value


def per_device(
    chips,
    reps,
    text_states,
    encoder_frames,
    out_cotangent,
    text_lengths,
    q_master,
    q_moment,
    q_second,
    key_weight,
    value_weight,
    out_weight,
):
    rows, width = q_master.shape
    depth = text_states.shape[1]
    chip_rows = CORES * rows
    index = lax.axis_index("dp")
    me = index.astype(jnp.int32).reshape(1)
    first = index % CORES == 0
    mates = [(i, i ^ 1) for i in range(CORES * chips)]
    swap = lambda a: lax.ppermute(a, "dp", mates)
    ring = 1 < chips <= RING_MOST and reps == 2
    right = lambda a: lax.ppermute(a, "dp", ring_pairs(chips, 1))
    left = lambda a: lax.ppermute(a, "dp", ring_pairs(chips, -1))
    same_core = [[CORES * i + c for i in range(chips)] for c in range(CORES)]

    in_use = jnp.arange(TOK, dtype=jnp.int32) < text_lengths[0]
    grad_out = jnp.where(in_use[:, None], out_cotangent, jnp.zeros_like(out_cotangent))
    x0, e0, g0 = text_states, encoder_frames, grad_out
    x1, e1, g1 = swap(x0), swap(e0), swap(g0)

    if ring:
        keep, send = pl.pallas_call(
            pack_kernel,
            out_shape=(jax.ShapeDtypeStruct((rows, 4 * WIDE), BF),) * 2,
            in_specs=[SM] + [HBM] * 4,
            out_specs=(VM, VM),
            scratch_shapes=[pltpu.VMEM((rows, width), F32)]
            + [pltpu.VMEM((rows, width), BF)] * 3
            + [pltpu.SemaphoreType.DMA((4,))],
            compiler_params=SMALL,
        )(me, q_master, key_weight, value_weight, out_weight.T)
        got, x1, e1, g1 = lax.optimization_barrier((swap(send), x1, e1, g1))
        pair = pl.pallas_call(
            join_kernel,
            out_shape=(jax.ShapeDtypeStruct((chip_rows, 2 * WIDE), BF),) * 2,
            in_specs=[SM] + [VM] * 2,
            out_specs=(VM, VM),
            compiler_params=SMALL,
        )(me, keep, got)
    else:
        parts = (q_master.astype(BF), key_weight, value_weight, out_weight.T)
        packs = [
            jnp.concatenate([w[:, c * WIDE : (c + 1) * WIDE] for w in parts], axis=1)
            for c in range(CORES)
        ]
        keep = jnp.where(first, packs[0], packs[1])
        got = swap(jnp.where(first, packs[1], packs[0]))
        block = jnp.where(
            first, jnp.concatenate([keep, got], axis=0), jnp.concatenate([got, keep], axis=0)
        )
        pair = (block[:, : 2 * WIDE], block[:, 2 * WIDE :])

    acts = (x0, x1, e0, e1, g0, g1, turn(x0), turn(x1))
    if ring:
        far = chips // 2
        steps, blocks = [0], list(pair)
        r = l = pair
        for k in range(1, far):
            r, l = [right(a) for a in r], [left(a) for a in l]
            steps += [chips - k, k]
            blocks += r + l
        steps += [far]
        blocks += [right(r[0]), left(l[1])]
        order = [(k, h * rows) for k in range(far, -1, -1) for h in range(2)]
        order += [(chips - k, h * rows) for k in range(far - 1, 0, -1) for h in range(2)]
        share, ctx_own, *sums = heads(chips, me, blocks, steps, acts, order, rows)
        term = dict(zip(order, sums))
        moves = {}
        for h, (away, back) in ((0, (right, left)), (1, (left, right))):
            sign = 1 if h == 0 else -1
            moves[h] = [away(term[far, h * rows]), back(term[(-sign * (far - 1)) % chips, h * rows])]
        for k in range(far - 1, 0, -1):
            for h, (away, back) in ((0, (right, left)), (1, (left, right))):
                sign = 1 if h == 0 else -1
                a, b = moves[h]
                if k > 1:
                    a = a + term[(sign * k) % chips, h * rows]
                    b = b + term[(-sign * (k - 1)) % chips, h * rows]
                    moves[h] = [away(a), back(b)]
                else:
                    moves[h] = [away(a + term[sign % chips, h * rows]), b]
        keep, send = pl.pallas_call(
            total_kernel,
            out_shape=(jax.ShapeDtypeStruct((rows, WIDE), F32),) * 2,
            in_specs=[SM] + [VM] * 6,
            out_specs=(VM, VM),
            compiler_params=SMALL,
        )(me, term[0, 0], *moves[0], term[0, rows], *moves[1])
        both = ("dp", "rep")
        across = [(i * reps + y, i * reps + (1 - y)) for i in range(CORES * chips) for y in range(reps)]
        cross = [(i * reps + y, (i ^ 1) * reps + (1 - y)) for i in range(CORES * chips) for y in range(reps)]
        got = swap(send)
        keep_y = lax.ppermute(keep, both, across)
        got_y = lax.ppermute(send, both, cross)
    else:
        blocks = [
            lax.all_gather(a, "dp", axis=0, tiled=True, axis_index_groups=same_core) for a in pair
        ]
        share, ctx_own, total = heads(chips, me, blocks, [0], acts, [(0, 0)], depth)
        total = lax.psum_scatter(
            total, "dp", scatter_dimension=0, tiled=True, axis_index_groups=same_core
        )
        keep = jnp.where(first, total[:rows], total[rows:])
        got = swap(jnp.where(first, total[rows:], total[:rows]))
        summed = jnp.where(
            first, jnp.concatenate([keep, got], axis=1), jnp.concatenate([got, keep], axis=1)
        )
        summed = lax.psum(summed, "rep")

    block_out = pl.pallas_call(
        out_kernel,
        out_shape=jax.ShapeDtypeStruct((TOK, depth), BF),
        in_specs=[VM] * 3,
        out_specs=VM,
        compiler_params=pltpu.CompilerParams(vmem_limit_bytes=8 * 2**20),
        cost_estimate=pl.CostEstimate(
            flops=2 * TOK * width * depth, bytes_accessed=4 * 10**6, transcendentals=0
        ),
    )(ctx_own, share, swap(share))
    if ring:
        got, keep_y, got_y, block_out = lax.optimization_barrier((got, keep_y, got_y, block_out))
        results = pl.pallas_call(
            step_kernel,
            out_shape=(jax.ShapeDtypeStruct((rows, width), F32),) * 4,
            in_specs=[SM] + [VM] * 7,
            out_specs=(VM,) * 4,
            compiler_params=SMALL,
        )(me, keep, keep_y, got, got_y, q_master, q_moment, q_second)
    else:
        results = adam(q_master, q_moment, q_second, summed)
    return (block_out, *results)


def solution(mesh):
    in_specs = (
        P(("dp", "rep"), None),
        P(("dp", "rep"), None),
        P(("dp", "rep"), None),
        P(("dp", "rep")),
        P("dp", None),
        P("dp", None),
        P("dp", None),
        P("dp", None),
        P("dp", None),
        P(None, "dp"),
    )
    out_specs = (P(("dp", "rep"), None), P("dp", None), P("dp", None), P("dp", None), P("dp", None))
    return jax.shard_map(
        functools.partial(per_device, mesh.shape["dp"] // CORES, mesh.shape["rep"]),
        mesh=mesh,
        in_specs=in_specs,
        out_specs=out_specs,
        check_vma=False,
    )
```

```python
import functools

import jax
import jax.numpy as jnp
from jax import lax
from jax.experimental import pallas as pl
from jax.experimental.pallas import tpu as pltpu
from jax.sharding import PartitionSpec as P

HEADS = 10
HEAD_DIM = 64
TOK = 448
CORES = 2
CORE_HEADS = HEADS // CORES
WIDE = CORE_HEADS * HEAD_DIM
CHAINS = 2
RING_MOST = 8

first_fix = 0.9999734386011124
second_fix = 0.8673804441052468
BF = jnp.bfloat16
F32 = jnp.float32
VM = pl.BlockSpec(memory_space=pltpu.VMEM)
SM = pl.BlockSpec(memory_space=pltpu.SMEM)
ANY = pl.BlockSpec(memory_space=pl.ANY)
HBM = pl.BlockSpec(memory_space=pltpu.HBM)
SMALL = pltpu.CompilerParams(vmem_limit_bytes=4 * 2**20)


ROWS = ((1,), (1,))


def padded(width):
    return -(-width // 128) * 128


def dot(a, b, dims=((1,), (0,))):
    return lax.dot_general(a, b, (dims, ((), ())), preferred_element_type=F32)


def ring_order(chips):
    return list(range(0, chips, 2)) + list(range(chips - 1, 0, -2))


def ring_pairs(chips, step):
    order = ring_order(chips)
    return [
        (CORES * order[i] + c, CORES * order[(i + step) % chips] + c)
        for i in range(chips)
        for c in range(CORES)
    ]


def chip_at(me_ref, chips, step):
    chip = me_ref[0] // CORES
    odd = chip % 2
    place = (1 - odd) * (chip // 2) + odd * (chips - 1 - chip // 2)
    place = (place + step + chips) % chips
    back = (place >= chips // 2).astype(jnp.int32)
    return (1 - back) * (2 * place) + back * (2 * (chips - 1 - place) + 1)


def pack(parts, core):
    return jnp.concatenate([w[:, core * WIDE : (core + 1) * WIDE] for w in parts], axis=1)


def pack_kernel(me, q, k, v, o, keep, send, qv, kv, vv, ov, sem):
    copies = [
        pltpu.make_async_copy(src, dst, sem.at[i])
        for i, (src, dst) in enumerate(((q, qv), (k, kv), (v, vv), (o, ov)))
    ]
    for c in copies:
        c.start()
    for c in copies:
        c.wait()
    first = me[0] % CORES == 0
    parts = (qv[...].astype(BF), kv[...], vv[...], ov[...])
    halves = [pack(parts, c) for c in range(CORES)]

    @pl.when(first)
    def _():
        keep[...] = halves[0]
        send[...] = halves[1]

    @pl.when(jnp.logical_not(first))
    def _():
        keep[...] = halves[1]
        send[...] = halves[0]


def turn_kernel(x, t):
    t[...] = x[...].T


def turn(x):
    return pl.pallas_call(
        turn_kernel,
        out_shape=jax.ShapeDtypeStruct(x.shape[::-1], BF),
        in_specs=[VM],
        out_specs=VM,
        compiler_params=pltpu.CompilerParams(vmem_limit_bytes=8 * 2**20),
        cost_estimate=pl.CostEstimate(flops=0, bytes_accessed=5 * 10**6, transcendentals=0),
    )(x)


def join_kernel(me, keep, got, *blocks):
    core = me[0] % CORES
    rows = keep.shape[0]
    mine = pl.ds(pl.multiple_of(core * rows, rows), rows)
    other = pl.ds(pl.multiple_of((1 - core) * rows, rows), rows)
    at = 0
    for block in blocks:
        cols = slice(at, at + block.shape[1])
        block[mine, :] = keep[:, cols]
        block[other, :] = got[:, cols]
        at += block.shape[1]


def head_kernel(chips, steps, pieces, *refs):
    refs = list(refs)
    take = lambda n: [refs.pop(0) for _ in range(n)]
    (me,) = take(1)
    chains = [take(len(s)) for s in steps]
    x0, x1, e0, e1, g0, g1, t0, t1 = take(8)
    share, ctx_own = take(2)
    sums = take(len(pieces))
    (w,) = take(1)
    number, width = CORE_HEADS, WIDE
    chip_rows = w.shape[0] // chips
    if len(steps[0]) == 1:
        places = [0]
    else:
        places = [pl.multiple_of(chip_at(me, chips, k) * chip_rows, chip_rows) for k in range(chips)]
    cols = w.shape[1] // len(chains)
    for i, blocks in enumerate(chains):
        for k, block in zip(steps[i], blocks):
            w[pl.ds(places[k], block.shape[0]), i * cols : (i + 1) * cols] = block[...]

    acts = ((x0, e0, g0), (x1, e1, g1))
    rows_of = []
    for xs, es, gs in acts:
        q = (dot(xs[...], w[:, :width]) * 0.125).astype(BF)
        kv = dot(es[...], w[:, width : 3 * width]).astype(BF)
        g = dot(gs[...], w[:, 3 * width :]).astype(BF)
        k, v = kv[:, :width], kv[:, width:]
        rows_of.append((q, k, v, g, k.T, v.T, g.T))

    def begin(clip, h):
        q, k, v, g, _, _, _ = rows_of[clip]
        cols = slice(h * HEAD_DIM, (h + 1) * HEAD_DIM)
        return dot(k[:, cols], q[:, cols], ROWS), dot(v[:, cols], g[:, cols], ROWS)

    def finish(clip, h, scores, grad_attention):
        _, _, _, _, kt, vt, gt = rows_of[clip]
        cols = slice(h * HEAD_DIM, (h + 1) * HEAD_DIM)
        e = jnp.exp(scores - jnp.max(scores, axis=0, keepdims=True))
        attention = (e * (1.0 / jnp.sum(e, axis=0, keepdims=True))).astype(BF)
        ctx = dot(vt[cols], attention)
        inner = jnp.sum(gt[cols].astype(F32) * ctx, axis=0, keepdims=True)
        grad_scores = (attention.astype(F32) * (grad_attention - inner)).astype(BF)
        return ctx.astype(BF), (dot(kt[cols], grad_scores) * 0.125).astype(BF)

    items = [(clip, h) for clip in range(2) for h in range(number)]
    begun = begin(*items[0])
    done = []
    for i, item in enumerate(items):
        now = begun
        if i + 1 < len(items):
            begun = begin(*items[i + 1])
        done.append(finish(*item, *now))
    ctx_own[...] = jnp.concatenate([c for c, _ in done[:number]], axis=0).T
    share[:TOK, :width] = jnp.concatenate([c for c, _ in done[number:]], axis=0).T
    share[TOK:, :width] = w[:, 3 * width :]
    grads = [
        jnp.concatenate([g for _, g in done[c * number : (c + 1) * number]], axis=0) for c in (0, 1)
    ]
    for out, (k, skip) in zip(sums, pieces):
        rows = pl.ds(places[k] + skip, out.shape[0])
        out[...] = dot(t0[rows, :], grads[0], ROWS) + dot(t1[rows, :], grads[1], ROWS)


def heads(chips, me, chains, steps, acts, pieces, piece_rows):
    depth = acts[6].shape[0]
    width = WIDE
    blocks = [b for chain in chains for b in chain]
    return pl.pallas_call(
        functools.partial(head_kernel, chips, steps, pieces),
        out_shape=(
            jax.ShapeDtypeStruct((TOK + depth, padded(width)), BF),
            jax.ShapeDtypeStruct((TOK, width), BF),
        )
        + (jax.ShapeDtypeStruct((piece_rows, width), F32),) * len(pieces),
        in_specs=[SM] + [VM] * (len(blocks) + 8),
        out_specs=(VM,) * (2 + len(pieces)),
        scratch_shapes=[pltpu.VMEM((depth, 4 * width), BF)],
        compiler_params=pltpu.CompilerParams(vmem_limit_bytes=16 * 2**20),
        cost_estimate=pl.CostEstimate(
            flops=9 * 10**9, bytes_accessed=15 * 10**6, transcendentals=2 * 10**6
        ),
    )(me, *blocks, *acts)


def out_kernel(ctx_own, share, got, out):
    out[...] = (
        dot(ctx_own[...], share[TOK:, :WIDE], ROWS) + dot(got[:TOK, :WIDE], got[TOK:, :WIDE], ROWS)
    ).astype(BF)


def total_kernel(me, *refs):
    *parts, keep, send = refs
    halves = [parts[i][...] + parts[i + 1][...] + parts[i + 2][...] for i in (0, 3)]
    for c in range(CORES):

        @pl.when(me[0] % CORES == c)
        def _():
            keep[...] = halves[c]
            send[...] = halves[1 - c]


def adam(q_master, q_moment, q_second, summed):
    q_gradient = summed * (1.0 / TOK)
    new_moment = 0.9 * q_moment + 0.1 * q_gradient
    new_second = 0.98 * q_second + 0.02 * q_gradient * q_gradient
    update = new_moment / first_fix / (jnp.sqrt(new_second / second_fix) + 1e-06)
    new_master = q_master - 0.001 * (update + 0.01 * q_master)
    return q_gradient, new_master, new_moment, new_second


def step_kernel(me, keep, keep_y, got, got_y, master, moment, second, *outs):
    core = me[0] % CORES
    mine = keep[...] + keep_y[...]
    other = got[...] + got_y[...]
    for c in range(CORES):

        @pl.when(core == c)
        def _():
            summed = jnp.concatenate([mine, other] if c == 0 else [other, mine], axis=1)
            for out, value in zip(outs, adam(master[...], moment[...], second[...], summed)):
                out[...] = value


def per_device(
    chips,
    reps,
    text_states,
    encoder_frames,
    out_cotangent,
    text_lengths,
    q_master,
    q_moment,
    q_second,
    key_weight,
    value_weight,
    out_weight,
):
    rows, width = q_master.shape
    depth = text_states.shape[1]
    chip_rows = CORES * rows
    index = lax.axis_index("dp")
    me = index.astype(jnp.int32).reshape(1)
    first = index % CORES == 0
    mates = [(i, i ^ 1) for i in range(CORES * chips)]
    swap = lambda a: lax.ppermute(a, "dp", mates)
    ring = 1 < chips <= RING_MOST and reps == 2
    right = lambda a: lax.ppermute(a, "dp", ring_pairs(chips, 1))
    left = lambda a: lax.ppermute(a, "dp", ring_pairs(chips, -1))
    same_core = [[CORES * i + c for i in range(chips)] for c in range(CORES)]

    in_use = jnp.arange(TOK, dtype=jnp.int32) < text_lengths[0]
    grad_out = jnp.where(in_use[:, None], out_cotangent, jnp.zeros_like(out_cotangent))
    x0, e0, g0 = text_states, encoder_frames, grad_out
    x1, e1, g1 = swap(x0), swap(e0), swap(g0)

    if ring:
        keep, send = pl.pallas_call(
            pack_kernel,
            out_shape=(jax.ShapeDtypeStruct((rows, 4 * WIDE), BF),) * 2,
            in_specs=[SM] + [HBM] * 4,
            out_specs=(VM, VM),
            scratch_shapes=[pltpu.VMEM((rows, width), F32)]
            + [pltpu.VMEM((rows, width), BF)] * 3
            + [pltpu.SemaphoreType.DMA((4,))],
            compiler_params=SMALL,
        )(me, q_master, key_weight, value_weight, out_weight.T)
        got, x1, e1, g1 = lax.optimization_barrier((swap(send), x1, e1, g1))
        own_blocks = pl.pallas_call(
            join_kernel,
            out_shape=(jax.ShapeDtypeStruct((chip_rows, 4 * WIDE // CHAINS), BF),) * CHAINS,
            in_specs=[SM] + [VM] * 2,
            out_specs=(VM,) * CHAINS,
            compiler_params=SMALL,
        )(me, keep, got)
    else:
        parts = (q_master.astype(BF), key_weight, value_weight, out_weight.T)
        packs = [pack(parts, c) for c in range(CORES)]
        keep = jnp.where(first, packs[0], packs[1])
        got = swap(jnp.where(first, packs[1], packs[0]))
        block = jnp.where(
            first, jnp.concatenate([keep, got], axis=0), jnp.concatenate([got, keep], axis=0)
        )
        own_blocks = [block]

    acts = (x0, x1, e0, e1, g0, g1, turn(x0), turn(x1))
    far = chips // 2
    if ring:
        steps, chains = [], []
        for i, own in enumerate(own_blocks):
            at, blocks = [0], [own]
            r = l = own
            for k in range(1, far):
                r, l = right(r), left(l)
                at += [chips - k, k]
                blocks += [r, l]
            at += [far]
            blocks += [right(r) if i % 2 == 0 else left(l)]
            steps.append(at)
            chains.append(blocks)
        pieces = [(k, h * rows) for k in range(far, 0, -1) for h in range(2)]
        pieces += [(chips - k, h * rows) for k in range(far - 1, 0, -1) for h in range(2)]
        pieces += [(0, h * rows) for h in range(2)]
        share, ctx_own, *sums = heads(chips, me, chains, steps, acts, pieces, rows)
        got_share = swap(share)
        totals = []
        for h in range(2):
            term = {k: s for (k, skip), s in zip(pieces, sums) if skip == h * rows}
            away, back, sign = (right, left, 1) if h == 0 else (left, right, -1)
            a, b = away(term[far]), back(term[-sign * (far - 1) % chips])
            for k in range(far - 1, 0, -1):
                a = away(a + term[sign * k % chips])
                if k > 1:
                    b = back(b + term[-sign * (k - 1) % chips])
            totals += [term[0], a, b]
        keep, send = pl.pallas_call(
            total_kernel,
            out_shape=(jax.ShapeDtypeStruct((rows, WIDE), F32),) * 2,
            in_specs=[SM] + [VM] * len(totals),
            out_specs=(VM, VM),
            compiler_params=SMALL,
        )(me, *totals)
        both = ("dp", "rep")
        across = [(i * reps + y, i * reps + (1 - y)) for i in range(CORES * chips) for y in range(reps)]
        cross = [(i * reps + y, (i ^ 1) * reps + (1 - y)) for i in range(CORES * chips) for y in range(reps)]
        got = swap(send)
        keep_y = lax.ppermute(keep, both, across)
        got_y = lax.ppermute(send, both, cross)
    else:
        block = lax.all_gather(own_blocks[0], "dp", axis=0, tiled=True, axis_index_groups=same_core)
        share, ctx_own, total = heads(chips, me, [[block]], [[0]], acts, [(0, 0)], depth)
        got_share = swap(share)
        total = lax.psum_scatter(
            total, "dp", scatter_dimension=0, tiled=True, axis_index_groups=same_core
        )
        keep = jnp.where(first, total[:rows], total[rows:])
        got = swap(jnp.where(first, total[rows:], total[:rows]))
        summed = jnp.where(
            first, jnp.concatenate([keep, got], axis=1), jnp.concatenate([got, keep], axis=1)
        )
        summed = lax.psum(summed, "rep")

    block_out = pl.pallas_call(
        out_kernel,
        out_shape=jax.ShapeDtypeStruct((TOK, depth), BF),
        in_specs=[VM] * 3,
        out_specs=VM,
        compiler_params=pltpu.CompilerParams(vmem_limit_bytes=8 * 2**20),
        cost_estimate=pl.CostEstimate(
            flops=2 * TOK * width * depth, bytes_accessed=4 * 10**6, transcendentals=0
        ),
    )(ctx_own, share, got_share)
    if ring:
        got, keep_y, got_y, block_out = lax.optimization_barrier((got, keep_y, got_y, block_out))
        results = pl.pallas_call(
            step_kernel,
            out_shape=(jax.ShapeDtypeStruct((rows, width), F32),) * 4,
            in_specs=[SM] + [VM] * 7,
            out_specs=(VM,) * 4,
            compiler_params=SMALL,
        )(me, keep, keep_y, got, got_y, q_master, q_moment, q_second)
    else:
        results = adam(q_master, q_moment, q_second, summed)
    return (block_out, *results)


def solution(mesh):
    in_specs = (
        P(("dp", "rep"), None),
        P(("dp", "rep"), None),
        P(("dp", "rep"), None),
        P(("dp", "rep")),
        P("dp", None),
        P("dp", None),
        P("dp", None),
        P("dp", None),
        P("dp", None),
        P(None, "dp"),
    )
    out_specs = (P(("dp", "rep"), None), P("dp", None), P("dp", None), P("dp", None), P("dp", None))
    return jax.shard_map(
        functools.partial(per_device, mesh.shape["dp"] // CORES, mesh.shape["rep"]),
        mesh=mesh,
        in_specs=in_specs,
        out_specs=out_specs,
        check_vma=False,
    )
```

```python
import functools

import jax
import jax.numpy as jnp
from jax import lax
from jax.experimental import pallas as pl
from jax.experimental.pallas import tpu as pltpu
from jax.sharding import PartitionSpec as P

HEADS = 10
HEAD_DIM = 64
TOK = 448
CORES = 2
CORE_HEADS = HEADS // CORES
WIDE = CORE_HEADS * HEAD_DIM
CHAINS = 2
RING_MOST = 8

first_fix = 0.9999734386011124
second_fix = 0.8673804441052468
BF = jnp.bfloat16
F32 = jnp.float32
VM = pl.BlockSpec(memory_space=pltpu.VMEM)
SM = pl.BlockSpec(memory_space=pltpu.SMEM)
ANY = pl.BlockSpec(memory_space=pl.ANY)
LARGE = pltpu.CompilerParams(vmem_limit_bytes=56 * 2**20)
HBM = pl.BlockSpec(memory_space=pltpu.HBM)
SMALL = pltpu.CompilerParams(vmem_limit_bytes=4 * 2**20)


ROWS = ((1,), (1,))


def padded(width):
    return -(-width // 128) * 128


def dot(a, b, dims=((1,), (0,))):
    return lax.dot_general(a, b, (dims, ((), ())), preferred_element_type=F32)


def ring_order(chips):
    return list(range(0, chips, 2)) + list(range(chips - 1, 0, -2))


def ring_pairs(chips, step):
    order = ring_order(chips)
    return [
        (CORES * order[i] + c, CORES * order[(i + step) % chips] + c)
        for i in range(chips)
        for c in range(CORES)
    ]


def chip_at(me_ref, chips, step):
    chip = me_ref[0] // CORES
    odd = chip % 2
    place = (1 - odd) * (chip // 2) + odd * (chips - 1 - chip // 2)
    place = (place + step + chips) % chips
    back = (place >= chips // 2).astype(jnp.int32)
    return (1 - back) * (2 * place) + back * (2 * (chips - 1 - place) + 1)


def pack(parts, core):
    return jnp.concatenate([w[:, core * WIDE : (core + 1) * WIDE] for w in parts], axis=1)


def pack_kernel(me, q, k, v, o, keep, send, qv, kv, vv, ov, sem):
    moves = ((q, qv), (k, kv), (v, vv), (o, ov))
    copies = [pltpu.make_async_copy(src, dst, sem.at[i]) for i, (src, dst) in enumerate(moves)]
    for c in copies:
        c.start()
    for c in copies:
        c.wait()
    first = me[0] % CORES == 0
    parts = (qv[...].astype(BF), kv[...], vv[...], ov[...])
    halves = [pack(parts, c) for c in range(CORES)]

    @pl.when(first)
    def _():
        keep[...] = halves[0]
        send[...] = halves[1]

    @pl.when(jnp.logical_not(first))
    def _():
        keep[...] = halves[1]
        send[...] = halves[0]


def stage_kernel(length, x, e, g, _, acts, xv, ev, gv, sem):
    parts = list(zip((x, e, g), (xv, ev, gv), act_rows(e.shape[0])))
    loads = [pltpu.make_async_copy(a, v, sem.at[i]) for i, (a, v, _) in enumerate(parts)]
    stores = [pltpu.make_async_copy(v, acts.at[at], sem.at[3 + i]) for i, (_, v, at) in enumerate(parts)]
    for c in loads[::-1]:
        c.start()
    loads[2].wait()
    in_use = lax.broadcasted_iota(jnp.int32, gv.shape, 0) < length[0]
    gv[...] = jnp.where(in_use, gv[...].astype(F32), 0.0).astype(BF)
    stores[2].start()
    for i in (1, 0):
        loads[i].wait()
        stores[i].start()
    for c in stores:
        c.wait()


def act_rows(frames):
    return pl.ds(0, TOK), pl.ds(TOK, frames), pl.ds(TOK + frames, TOK)


def turn_kernel(mine, other, t0, t1):
    t0[...] = mine[:TOK, :].T
    t1[...] = other[:TOK, :].T


def turn(mine, other):
    return pl.pallas_call(
        turn_kernel,
        out_shape=(jax.ShapeDtypeStruct((mine.shape[1], TOK), BF),) * 2,
        in_specs=[VM] * 2,
        out_specs=(VM,) * 2,
        compiler_params=pltpu.CompilerParams(vmem_limit_bytes=8 * 2**20),
        cost_estimate=pl.CostEstimate(flops=0, bytes_accessed=5 * 10**6, transcendentals=0),
    )(mine, other)


def join_kernel(me, keep, got, *blocks):
    core = me[0] % CORES
    rows = keep.shape[0]
    mine = pl.ds(pl.multiple_of(core * rows, rows), rows)
    other = pl.ds(pl.multiple_of((1 - core) * rows, rows), rows)
    at = 0
    for block in blocks:
        cols = slice(at, at + block.shape[1])
        block[mine, :] = keep[:, cols]
        block[other, :] = got[:, cols]
        at += block.shape[1]


def head_kernel(chips, steps, pieces, *refs):
    refs = list(refs)
    take = lambda n: [refs.pop(0) for _ in range(n)]
    (me,) = take(1)
    chains = [take(len(s)) for s in steps]
    mine, other, t0, t1 = take(4)
    share, ctx_own = take(2)
    sums = take(len(pieces))
    w, loaded, whole, sem = take(4)
    load = pltpu.make_async_copy(other, loaded, sem)
    load.start()
    number, width = CORE_HEADS, WIDE
    chip_rows = w.shape[0] // chips
    if len(steps[0]) == 1:
        places = [0]
    else:
        places = [pl.multiple_of(chip_at(me, chips, k) * chip_rows, chip_rows) for k in range(chips)]
    cols = w.shape[1] // len(chains)
    for i, blocks in enumerate(chains):
        for k, block in zip(steps[i], blocks):
            w[pl.ds(places[k], block.shape[0]), i * cols : (i + 1) * cols] = block[...]

    x_at, e_at, g_at = act_rows(mine.shape[0] - 2 * TOK)
    rows_of = []

    def project(clip):
        acts = (mine, loaded)[clip]
        if clip == 1:
            load.wait()
        q = (dot(acts[x_at, :], w[:, :width]) * 0.125).astype(BF)
        kv = dot(acts[e_at, :], w[:, width : 3 * width]).astype(BF)
        g = dot(acts[g_at, :], w[:, 3 * width :]).astype(BF)
        k, v = kv[:, :width], kv[:, width:]
        rows_of.append((q, k, v, g, k.T, v.T, g.T))

    def begin(clip, h):
        q, k, v, g, _, _, _ = rows_of[clip]
        cols = slice(h * HEAD_DIM, (h + 1) * HEAD_DIM)
        return dot(k[:, cols], q[:, cols], ROWS), dot(v[:, cols], g[:, cols], ROWS)

    def finish(clip, h, scores, grad_attention):
        _, _, _, _, kt, vt, gt = rows_of[clip]
        cols = slice(h * HEAD_DIM, (h + 1) * HEAD_DIM)
        e = jnp.exp(scores - jnp.max(scores, axis=0, keepdims=True))
        attention = (e * (1.0 / jnp.sum(e, axis=0, keepdims=True))).astype(BF)
        ctx = dot(vt[cols], attention)
        inner = jnp.sum(gt[cols].astype(F32) * ctx, axis=0, keepdims=True)
        grad_scores = (attention.astype(F32) * (grad_attention - inner)).astype(BF)
        return ctx.astype(BF), (dot(kt[cols], grad_scores) * 0.125).astype(BF)

    items = [(clip, h) for clip in range(2) for h in range(number)]
    project(0)
    begun = begin(*items[0])
    done = []
    for i, item in enumerate(items):
        now = begun
        if i == 1:
            project(1)
        if i + 1 < len(items):
            begun = begin(*items[i + 1])
        done.append(finish(*item, *now))
    ctx_own[...] = jnp.concatenate([c for c, _ in done[:number]], axis=0).T
    share[:TOK, :width] = jnp.concatenate([c for c, _ in done[number:]], axis=0).T
    share[TOK:, :width] = w[:, 3 * width :]
    grads = [
        jnp.concatenate([g for _, g in done[c * number : (c + 1) * number]], axis=0) for c in (0, 1)
    ]
    whole[...] = dot(t0[...], grads[0].T) + dot(t1[...], grads[1].T)
    for out, (k, skip) in zip(sums, pieces):
        fold = out.shape[1] // width
        for i in range(fold):
            rows = pl.ds(places[k] + skip + i * out.shape[0], out.shape[0])
            out[:, i * width : (i + 1) * width] = whole[rows, :]


def heads(chips, me, chains, steps, acts, pieces, piece_shape):
    depth = acts[0].shape[1]
    width = WIDE
    blocks = [b for chain in chains for b in chain]
    return pl.pallas_call(
        functools.partial(head_kernel, chips, steps, pieces),
        out_shape=(
            jax.ShapeDtypeStruct((TOK + depth, padded(width)), BF),
            jax.ShapeDtypeStruct((TOK, width), BF),
        )
        + (jax.ShapeDtypeStruct(piece_shape, F32),) * len(pieces),
        in_specs=[SM] + [VM] * len(blocks) + [VM, ANY, VM, VM],
        out_specs=(VM,) * (2 + len(pieces)),
        scratch_shapes=[pltpu.VMEM((depth, 4 * width), BF)]
        + [pltpu.VMEM(acts[1].shape, BF), pltpu.VMEM((depth, width), F32), pltpu.SemaphoreType.DMA],
        compiler_params=pltpu.CompilerParams(vmem_limit_bytes=22 * 2**20),
        cost_estimate=pl.CostEstimate(
            flops=9 * 10**9, bytes_accessed=15 * 10**6, transcendentals=2 * 10**6
        ),
    )(me, *blocks, *acts)


def out_kernel(ctx_own, share, got, out):
    out[...] = (
        dot(ctx_own[...], share[TOK:, :WIDE], ROWS) + dot(got[:TOK, :WIDE], got[TOK:, :WIDE], ROWS)
    ).astype(BF)


def total_kernel(me, *refs):
    *parts, keep, send = refs
    halves = [parts[i][...] + parts[i + 1][...] + parts[i + 2][...] for i in (0, 3)]
    for c in range(CORES):

        @pl.when(me[0] % CORES == c)
        def _():
            keep[...] = halves[c]
            send[...] = halves[1 - c]


def adam(q_master, q_moment, q_second, summed):
    q_gradient = summed * (1.0 / TOK)
    new_moment = 0.9 * q_moment + 0.1 * q_gradient
    new_second = 0.98 * q_second + 0.02 * q_gradient * q_gradient
    update = new_moment / first_fix / (jnp.sqrt(new_second / second_fix) + 1e-06)
    new_master = q_master - 0.001 * (update + 0.01 * q_master)
    return q_gradient, new_master, new_moment, new_second


def step_kernel(me, keep, keep_y, got, got_y, master, moment, second, *outs):
    core = me[0] % CORES
    mine = keep[...] + keep_y[...]
    other = got[...] + got_y[...]
    for c in range(CORES):

        @pl.when(core == c)
        def _():
            for i in range(2):
                rows = slice(i * mine.shape[0], (i + 1) * mine.shape[0])
                cols = slice(i * WIDE, (i + 1) * WIDE)
                halves = (mine[:, cols], other[:, cols])
                summed = jnp.concatenate([halves[c], halves[1 - c]], axis=1)
                values = adam(master[rows, :], moment[rows, :], second[rows, :], summed)
                for out, value in zip(outs, values):
                    out[rows, :] = value


def per_device(
    chips,
    reps,
    text_states,
    encoder_frames,
    out_cotangent,
    text_lengths,
    q_master,
    q_moment,
    q_second,
    key_weight,
    value_weight,
    out_weight,
):
    rows, width = q_master.shape
    frames, depth = encoder_frames.shape
    chip_rows = CORES * rows
    index = lax.axis_index("dp")
    me = index.astype(jnp.int32).reshape(1)
    first = index % CORES == 0
    mates = [(i, i ^ 1) for i in range(CORES * chips)]
    swap = lambda a: lax.ppermute(a, "dp", mates)
    ring = 1 < chips <= RING_MOST and reps == 2
    right = lambda a: lax.ppermute(a, "dp", ring_pairs(chips, 1))
    left = lambda a: lax.ppermute(a, "dp", ring_pairs(chips, -1))
    same_core = [[CORES * i + c for i in range(chips)] for c in range(CORES)]

    if ring:
        keep, send = pl.pallas_call(
            pack_kernel,
            out_shape=(jax.ShapeDtypeStruct((rows, 4 * WIDE), BF),) * 2,
            in_specs=[SM] + [HBM] * 4,
            out_specs=(VM,) * 2,
            scratch_shapes=[pltpu.VMEM((rows, width), F32)]
            + [pltpu.VMEM((rows, width), BF)] * 3
            + [pltpu.SemaphoreType.DMA((4,))],
            compiler_params=LARGE,
        )(me, q_master, key_weight, value_weight, out_weight.T)
        got = swap(send)
        mine = pl.pallas_call(
            stage_kernel,
            out_shape=jax.ShapeDtypeStruct((2 * TOK + frames, depth), BF),
            in_specs=[SM] + [HBM] * 3 + [ANY],
            out_specs=HBM,
            scratch_shapes=[pltpu.VMEM((n, depth), BF) for n in (TOK, frames, TOK)]
            + [pltpu.SemaphoreType.DMA((6,))],
            compiler_params=LARGE,
        )(text_lengths, text_states, encoder_frames, out_cotangent, keep)
        own_blocks = pl.pallas_call(
            join_kernel,
            out_shape=(jax.ShapeDtypeStruct((chip_rows, 4 * WIDE // CHAINS), BF),) * CHAINS,
            in_specs=[SM] + [VM] * 2,
            out_specs=(VM,) * CHAINS,
            compiler_params=SMALL,
        )(me, keep, got)
    else:
        parts = (q_master.astype(BF), key_weight, value_weight, out_weight.T)
        packs = [pack(parts, c) for c in range(CORES)]
        keep = jnp.where(first, packs[0], packs[1])
        got = swap(jnp.where(first, packs[1], packs[0]))
        block = jnp.where(
            first, jnp.concatenate([keep, got], axis=0), jnp.concatenate([got, keep], axis=0)
        )
        own_blocks = [block]
        in_use = jnp.arange(TOK, dtype=jnp.int32) < text_lengths[0]
        grad_out = jnp.where(in_use[:, None], out_cotangent, jnp.zeros_like(out_cotangent))
        mine = jnp.concatenate([text_states, encoder_frames, grad_out], axis=0)

    mine, *own_blocks = lax.optimization_barrier((mine, *own_blocks))
    other = swap(mine)
    acts = (mine, other, *turn(mine, other))
    far = chips // 2
    if ring:
        steps, chains = [], []
        for i, own in enumerate(own_blocks):
            at, blocks = [0], [own]
            r = l = own
            for k in range(1, far):
                r, l = right(r), left(l)
                at += [chips - k, k]
                blocks += [r, l]
            at += [far]
            blocks += [right(r) if i % 2 == 0 else left(l)]
            steps.append(at)
            chains.append(blocks)
        pieces = [(k, h * rows) for k in range(far, 0, -1) for h in range(2)]
        pieces += [(chips - k, h * rows) for k in range(far - 1, 0, -1) for h in range(2)]
        pieces += [(0, h * rows) for h in range(2)]
        share, ctx_own, *sums = heads(chips, me, chains, steps, acts, pieces, (rows // 2, 2 * WIDE))
        got_share = swap(share)
        totals = []
        for h in range(2):
            term = {k: s for (k, skip), s in zip(pieces, sums) if skip == h * rows}
            away, back, sign = (right, left, 1) if h == 0 else (left, right, -1)
            a, b = away(term[far]), back(term[-sign * (far - 1) % chips])
            for k in range(far - 1, 0, -1):
                a = away(a + term[sign * k % chips])
                if k > 1:
                    b = back(b + term[-sign * (k - 1) % chips])
            totals += [term[0], a, b]
        keep, send = pl.pallas_call(
            total_kernel,
            out_shape=(jax.ShapeDtypeStruct((rows // 2, 2 * WIDE), F32),) * 2,
            in_specs=[SM] + [VM] * len(totals),
            out_specs=(VM, VM),
            compiler_params=SMALL,
        )(me, *totals)
        both = ("dp", "rep")
        across = [(i * reps + y, i * reps + (1 - y)) for i in range(CORES * chips) for y in range(reps)]
        cross = [(i * reps + y, (i ^ 1) * reps + (1 - y)) for i in range(CORES * chips) for y in range(reps)]
        got = swap(send)
        keep_y = lax.ppermute(keep, both, across)
        got_y = lax.ppermute(send, both, cross)
    else:
        block = lax.all_gather(own_blocks[0], "dp", axis=0, tiled=True, axis_index_groups=same_core)
        share, ctx_own, total = heads(chips, me, [[block]], [[0]], acts, [(0, 0)], (depth, WIDE))
        got_share = swap(share)
        total = lax.psum_scatter(
            total, "dp", scatter_dimension=0, tiled=True, axis_index_groups=same_core
        )
        keep = jnp.where(first, total[:rows], total[rows:])
        got = swap(jnp.where(first, total[rows:], total[:rows]))
        summed = jnp.where(
            first, jnp.concatenate([keep, got], axis=1), jnp.concatenate([got, keep], axis=1)
        )
        summed = lax.psum(summed, "rep")

    block_out = pl.pallas_call(
        out_kernel,
        out_shape=jax.ShapeDtypeStruct((TOK, depth), BF),
        in_specs=[VM] * 3,
        out_specs=VM,
        compiler_params=pltpu.CompilerParams(vmem_limit_bytes=8 * 2**20),
        cost_estimate=pl.CostEstimate(
            flops=2 * TOK * width * depth, bytes_accessed=4 * 10**6, transcendentals=0
        ),
    )(ctx_own, share, got_share)
    if ring:
        got, keep_y, got_y, block_out = lax.optimization_barrier((got, keep_y, got_y, block_out))
        results = pl.pallas_call(
            step_kernel,
            out_shape=(jax.ShapeDtypeStruct((rows, width), F32),) * 4,
            in_specs=[SM] + [VM] * 7,
            out_specs=(VM,) * 4,
            compiler_params=SMALL,
        )(me, keep, keep_y, got, got_y, q_master, q_moment, q_second)
    else:
        results = adam(q_master, q_moment, q_second, summed)
    return (block_out, *results)


def solution(mesh):
    in_specs = (
        P(("dp", "rep"), None),
        P(("dp", "rep"), None),
        P(("dp", "rep"), None),
        P(("dp", "rep")),
        P("dp", None),
        P("dp", None),
        P("dp", None),
        P("dp", None),
        P("dp", None),
        P(None, "dp"),
    )
    out_specs = (P(("dp", "rep"), None), P("dp", None), P("dp", None), P("dp", None), P("dp", None))
    return jax.shard_map(
        functools.partial(per_device, mesh.shape["dp"] // CORES, mesh.shape["rep"]),
        mesh=mesh,
        in_specs=in_specs,
        out_specs=out_specs,
        check_vma=False,
    )
```

```python
import functools

import jax
import jax.numpy as jnp
from jax import lax
from jax.experimental import pallas as pl
from jax.experimental.pallas import tpu as pltpu
from jax.sharding import PartitionSpec as P

HEADS = 10
HEAD_DIM = 64
TOK = 448
CORES = 2
CORE_HEADS = HEADS // CORES
WIDE = CORE_HEADS * HEAD_DIM
CHAINS = 2
RING_MOST = 8

first_fix = 0.9999734386011124
second_fix = 0.8673804441052468
BF = jnp.bfloat16
F32 = jnp.float32
VM = pl.BlockSpec(memory_space=pltpu.VMEM)
SM = pl.BlockSpec(memory_space=pltpu.SMEM)
ANY = pl.BlockSpec(memory_space=pl.ANY)
LARGE = pltpu.CompilerParams(vmem_limit_bytes=56 * 2**20)
HBM = pl.BlockSpec(memory_space=pltpu.HBM)
SMALL = pltpu.CompilerParams(vmem_limit_bytes=4 * 2**20)


ROWS = ((1,), (1,))


def padded(width):
    return -(-width // 128) * 128


def dot(a, b, dims=((1,), (0,))):
    return lax.dot_general(a, b, (dims, ((), ())), preferred_element_type=F32)


def ring_order(chips):
    return list(range(0, chips, 2)) + list(range(chips - 1, 0, -2))


def ring_pairs(chips, step):
    order = ring_order(chips)
    return [
        (CORES * order[i] + c, CORES * order[(i + step) % chips] + c)
        for i in range(chips)
        for c in range(CORES)
    ]


def chip_at(me_ref, chips, step):
    chip = me_ref[0] // CORES
    odd = chip % 2
    place = (1 - odd) * (chip // 2) + odd * (chips - 1 - chip // 2)
    place = (place + step + chips) % chips
    back = (place >= chips // 2).astype(jnp.int32)
    return (1 - back) * (2 * place) + back * (2 * (chips - 1 - place) + 1)


def pack(parts, core):
    return jnp.concatenate([w[:, core * WIDE : (core + 1) * WIDE] for w in parts], axis=1)


def pack_kernel(me, q, k, v, o, keep, send, qv, kv, vv, ov, sem):
    moves = ((q, qv), (k, kv), (v, vv), (o, ov))
    copies = [pltpu.make_async_copy(src, dst, sem.at[i]) for i, (src, dst) in enumerate(moves)]
    for c in copies:
        c.start()
    for c in copies:
        c.wait()
    first = me[0] % CORES == 0
    parts = (qv[...].astype(BF), kv[...], vv[...], ov[...])
    halves = [pack(parts, c) for c in range(CORES)]

    @pl.when(first)
    def _():
        keep[...] = halves[0]
        send[...] = halves[1]

    @pl.when(jnp.logical_not(first))
    def _():
        keep[...] = halves[1]
        send[...] = halves[0]


def stage_kernel(length, x, e, g, _, acts, xv, ev, gv, sem):
    parts = list(zip((x, e, g), (xv, ev, gv), act_rows(e.shape[0])))
    loads = [pltpu.make_async_copy(a, v, sem.at[i]) for i, (a, v, _) in enumerate(parts)]
    stores = [pltpu.make_async_copy(v, acts.at[at], sem.at[3 + i]) for i, (_, v, at) in enumerate(parts)]
    for c in loads[::-1]:
        c.start()
    loads[2].wait()
    in_use = lax.broadcasted_iota(jnp.int32, gv.shape, 0) < length[0]
    gv[...] = jnp.where(in_use, gv[...].astype(F32), 0.0).astype(BF)
    stores[2].start()
    for i in (1, 0):
        loads[i].wait()
        stores[i].start()
    for c in stores:
        c.wait()


def act_rows(frames):
    return pl.ds(0, TOK), pl.ds(TOK, frames), pl.ds(TOK + frames, TOK)


def turn_kernel(mine, other, t0, t1):
    t0[...] = mine[:TOK, :].T
    t1[...] = other[:TOK, :].T


def turn(mine, other):
    return pl.pallas_call(
        turn_kernel,
        out_shape=(jax.ShapeDtypeStruct((mine.shape[1], TOK), BF),) * 2,
        in_specs=[VM] * 2,
        out_specs=(VM,) * 2,
        compiler_params=pltpu.CompilerParams(vmem_limit_bytes=8 * 2**20),
        cost_estimate=pl.CostEstimate(flops=0, bytes_accessed=5 * 10**6, transcendentals=0),
    )(mine, other)


def join_kernel(me, keep, got, *blocks):
    core = me[0] % CORES
    rows = keep.shape[0]
    mine = pl.ds(pl.multiple_of(core * rows, rows), rows)
    other = pl.ds(pl.multiple_of((1 - core) * rows, rows), rows)
    at = 0
    for block in blocks:
        cols = slice(at, at + block.shape[1])
        block[mine, :] = keep[:, cols]
        block[other, :] = got[:, cols]
        at += block.shape[1]


def head_kernel(chips, steps, pieces, *refs):
    refs = list(refs)
    take = lambda n: [refs.pop(0) for _ in range(n)]
    (me,) = take(1)
    chains = [take(len(s)) for s in steps]
    mine, other, t0, t1 = take(4)
    share, ctx_own = take(2)
    sums = take(len(pieces))
    w, whole = take(2)
    number, width = CORE_HEADS, WIDE
    chip_rows = w.shape[0] // chips
    if len(steps[0]) == 1:
        places = [0]
    else:
        places = [pl.multiple_of(chip_at(me, chips, k) * chip_rows, chip_rows) for k in range(chips)]
    cols = w.shape[1] // len(chains)
    for i, blocks in enumerate(chains):
        for k, block in zip(steps[i], blocks):
            w[pl.ds(places[k], block.shape[0]), i * cols : (i + 1) * cols] = block[...]

    x_at, e_at, g_at = act_rows(mine.shape[0] - 2 * TOK)
    rows_of = []

    def project(clip):
        acts = (mine, other)[clip]
        q = (dot(acts[x_at, :], w[:, :width]) * 0.125).astype(BF)
        kv = dot(acts[e_at, :], w[:, width : 3 * width]).astype(BF)
        g = dot(acts[g_at, :], w[:, 3 * width :]).astype(BF)
        k, v = kv[:, :width], kv[:, width:]
        rows_of.append((q, k, v, g, k.T, v.T, g.T))

    def begin(clip, h, tokens):
        q, k, v, g, _, _, _ = rows_of[clip]
        cols = slice(h * HEAD_DIM, (h + 1) * HEAD_DIM)
        return dot(k[:, cols], q[tokens, cols], ROWS), dot(v[:, cols], g[tokens, cols], ROWS)

    def finish(clip, h, tokens, scores, grad_attention):
        _, _, _, _, kt, vt, gt = rows_of[clip]
        cols = slice(h * HEAD_DIM, (h + 1) * HEAD_DIM)
        e = jnp.exp(scores - jnp.max(scores, axis=0, keepdims=True))
        attention = (e * (1.0 / jnp.sum(e, axis=0, keepdims=True))).astype(BF)
        ctx = dot(vt[cols], attention)
        inner = jnp.sum(gt[cols, tokens].astype(F32) * ctx, axis=0, keepdims=True)
        grad_scores = (attention.astype(F32) * (grad_attention - inner)).astype(BF)
        return ctx.astype(BF), (dot(kt[cols], grad_scores) * 0.125).astype(BF)

    halves = (slice(0, 256), slice(256, TOK))
    items = [(clip, h, t) for clip in range(2) for h in range(number) for t in halves]
    project(0)
    begun = [begin(*item) for item in items[:2]]
    done = []
    for i, item in enumerate(items):
        if i == 6:
            project(1)
        if i + 2 < len(items):
            begun.append(begin(*items[i + 2]))
        done.append(finish(*item, *begun[i]))
    ctxs, grads = [
        [
            jnp.concatenate(
                [
                    jnp.concatenate([done[(c * number + h) * 2 + t][which] for t in (0, 1)], axis=1)
                    for h in range(number)
                ],
                axis=0,
            ).T
            for c in (0, 1)
        ]
        for which in (0, 1)
    ]
    ctx_own[...] = ctxs[0]
    share[:TOK, :width] = ctxs[1]
    share[TOK:, :width] = w[:, 3 * width :]
    whole[...] = dot(t0[...], grads[0]) + dot(t1[...], grads[1])
    for out, (k, skip) in zip(sums, pieces):
        fold = out.shape[1] // width
        for i in range(fold):
            rows = pl.ds(places[k] + skip + i * out.shape[0], out.shape[0])
            out[:, i * width : (i + 1) * width] = whole[rows, :]


def heads(chips, me, chains, steps, acts, pieces, piece_shape):
    depth = acts[0].shape[1]
    width = WIDE
    blocks = [b for chain in chains for b in chain]
    return pl.pallas_call(
        functools.partial(head_kernel, chips, steps, pieces),
        out_shape=(
            jax.ShapeDtypeStruct((TOK + depth, padded(width)), BF),
            jax.ShapeDtypeStruct((TOK, width), BF),
        )
        + (jax.ShapeDtypeStruct(piece_shape, F32),) * len(pieces),
        in_specs=[SM] + [VM] * (len(blocks) + 4),
        out_specs=(VM,) * (2 + len(pieces)),
        scratch_shapes=[pltpu.VMEM((depth, 4 * width), BF)]
        + [pltpu.VMEM((depth, width), F32)],
        compiler_params=pltpu.CompilerParams(vmem_limit_bytes=22 * 2**20),
        cost_estimate=pl.CostEstimate(
            flops=9 * 10**9, bytes_accessed=15 * 10**6, transcendentals=2 * 10**6
        ),
    )(me, *blocks, *acts)


def out_kernel(ctx_own, share, got, out):
    out[...] = (
        dot(ctx_own[...], share[TOK:, :WIDE], ROWS) + dot(got[:TOK, :WIDE], got[TOK:, :WIDE], ROWS)
    ).astype(BF)


def total_kernel(me, *refs):
    *parts, keep, send = refs
    halves = [parts[i][...] + parts[i + 1][...] + parts[i + 2][...] for i in (0, 3)]
    for c in range(CORES):

        @pl.when(me[0] % CORES == c)
        def _():
            keep[...] = halves[c]
            send[...] = halves[1 - c]


def adam(q_master, q_moment, q_second, summed):
    q_gradient = summed * (1.0 / TOK)
    new_moment = 0.9 * q_moment + 0.1 * q_gradient
    new_second = 0.98 * q_second + 0.02 * q_gradient * q_gradient
    update = new_moment / first_fix / (jnp.sqrt(new_second / second_fix) + 1e-06)
    new_master = q_master - 0.001 * (update + 0.01 * q_master)
    return q_gradient, new_master, new_moment, new_second


def step_kernel(me, keep, keep_y, got, got_y, master, moment, second, *outs):
    core = me[0] % CORES
    mine = keep[...] + keep_y[...]
    other = got[...] + got_y[...]
    for c in range(CORES):

        @pl.when(core == c)
        def _():
            for i in range(2):
                rows = slice(i * mine.shape[0], (i + 1) * mine.shape[0])
                cols = slice(i * WIDE, (i + 1) * WIDE)
                halves = (mine[:, cols], other[:, cols])
                summed = jnp.concatenate([halves[c], halves[1 - c]], axis=1)
                values = adam(master[rows, :], moment[rows, :], second[rows, :], summed)
                for out, value in zip(outs, values):
                    out[rows, :] = value


def per_device(
    chips,
    reps,
    text_states,
    encoder_frames,
    out_cotangent,
    text_lengths,
    q_master,
    q_moment,
    q_second,
    key_weight,
    value_weight,
    out_weight,
):
    rows, width = q_master.shape
    frames, depth = encoder_frames.shape
    chip_rows = CORES * rows
    index = lax.axis_index("dp")
    me = index.astype(jnp.int32).reshape(1)
    first = index % CORES == 0
    mates = [(i, i ^ 1) for i in range(CORES * chips)]
    swap = lambda a: lax.ppermute(a, "dp", mates)
    ring = 1 < chips <= RING_MOST and reps == 2
    right = lambda a: lax.ppermute(a, "dp", ring_pairs(chips, 1))
    left = lambda a: lax.ppermute(a, "dp", ring_pairs(chips, -1))
    same_core = [[CORES * i + c for i in range(chips)] for c in range(CORES)]

    if ring:
        keep, send = pl.pallas_call(
            pack_kernel,
            out_shape=(jax.ShapeDtypeStruct((rows, 4 * WIDE), BF),) * 2,
            in_specs=[SM] + [HBM] * 4,
            out_specs=(VM,) * 2,
            scratch_shapes=[pltpu.VMEM((rows, width), F32)]
            + [pltpu.VMEM((rows, width), BF)] * 3
            + [pltpu.SemaphoreType.DMA((4,))],
            compiler_params=LARGE,
        )(me, q_master, key_weight, value_weight, out_weight.T)
        got = swap(send)
        mine = pl.pallas_call(
            stage_kernel,
            out_shape=jax.ShapeDtypeStruct((2 * TOK + frames, depth), BF),
            in_specs=[SM] + [HBM] * 3 + [ANY],
            out_specs=HBM,
            scratch_shapes=[pltpu.VMEM((n, depth), BF) for n in (TOK, frames, TOK)]
            + [pltpu.SemaphoreType.DMA((6,))],
            compiler_params=LARGE,
        )(text_lengths, text_states, encoder_frames, out_cotangent, keep)
        own_blocks = pl.pallas_call(
            join_kernel,
            out_shape=(jax.ShapeDtypeStruct((chip_rows, 4 * WIDE // CHAINS), BF),) * CHAINS,
            in_specs=[SM] + [VM] * 2,
            out_specs=(VM,) * CHAINS,
            compiler_params=SMALL,
        )(me, keep, got)
    else:
        parts = (q_master.astype(BF), key_weight, value_weight, out_weight.T)
        packs = [pack(parts, c) for c in range(CORES)]
        keep = jnp.where(first, packs[0], packs[1])
        got = swap(jnp.where(first, packs[1], packs[0]))
        block = jnp.where(
            first, jnp.concatenate([keep, got], axis=0), jnp.concatenate([got, keep], axis=0)
        )
        own_blocks = [block]
        in_use = jnp.arange(TOK, dtype=jnp.int32) < text_lengths[0]
        grad_out = jnp.where(in_use[:, None], out_cotangent, jnp.zeros_like(out_cotangent))
        mine = jnp.concatenate([text_states, encoder_frames, grad_out], axis=0)

    mine, *own_blocks = lax.optimization_barrier((mine, *own_blocks))
    other = swap(mine)
    acts = (mine, other, *turn(mine, other))
    far = chips // 2
    if ring:
        steps, chains = [], []
        for i, own in enumerate(own_blocks):
            at, blocks = [0], [own]
            r = l = own
            for k in range(1, far):
                r, l = right(r), left(l)
                at += [chips - k, k]
                blocks += [r, l]
            at += [far]
            blocks += [right(r) if i % 2 == 0 else left(l)]
            steps.append(at)
            chains.append(blocks)
        pieces = [(k, h * rows) for k in range(far, 0, -1) for h in range(2)]
        pieces += [(chips - k, h * rows) for k in range(far - 1, 0, -1) for h in range(2)]
        pieces += [(0, h * rows) for h in range(2)]
        share, ctx_own, *sums = heads(chips, me, chains, steps, acts, pieces, (rows // 2, 2 * WIDE))
        got_share = swap(share)
        totals = []
        for h in range(2):
            term = {k: s for (k, skip), s in zip(pieces, sums) if skip == h * rows}
            away, back, sign = (right, left, 1) if h == 0 else (left, right, -1)
            a, b = away(term[far]), back(term[-sign * (far - 1) % chips])
            for k in range(far - 1, 0, -1):
                a = away(a + term[sign * k % chips])
                if k > 1:
                    b = back(b + term[-sign * (k - 1) % chips])
            totals += [term[0], a, b]
        keep, send = pl.pallas_call(
            total_kernel,
            out_shape=(jax.ShapeDtypeStruct((rows // 2, 2 * WIDE), F32),) * 2,
            in_specs=[SM] + [VM] * len(totals),
            out_specs=(VM, VM),
            compiler_params=SMALL,
        )(me, *totals)
        both = ("dp", "rep")
        across = [(i * reps + y, i * reps + (1 - y)) for i in range(CORES * chips) for y in range(reps)]
        cross = [(i * reps + y, (i ^ 1) * reps + (1 - y)) for i in range(CORES * chips) for y in range(reps)]
        got = swap(send)
        keep_y = lax.ppermute(keep, both, across)
        got_y = lax.ppermute(send, both, cross)
    else:
        block = lax.all_gather(own_blocks[0], "dp", axis=0, tiled=True, axis_index_groups=same_core)
        share, ctx_own, total = heads(chips, me, [[block]], [[0]], acts, [(0, 0)], (depth, WIDE))
        got_share = swap(share)
        total = lax.psum_scatter(
            total, "dp", scatter_dimension=0, tiled=True, axis_index_groups=same_core
        )
        keep = jnp.where(first, total[:rows], total[rows:])
        got = swap(jnp.where(first, total[rows:], total[:rows]))
        summed = jnp.where(
            first, jnp.concatenate([keep, got], axis=1), jnp.concatenate([got, keep], axis=1)
        )
        summed = lax.psum(summed, "rep")

    block_out = pl.pallas_call(
        out_kernel,
        out_shape=jax.ShapeDtypeStruct((TOK, depth), BF),
        in_specs=[VM] * 3,
        out_specs=VM,
        compiler_params=pltpu.CompilerParams(vmem_limit_bytes=8 * 2**20),
        cost_estimate=pl.CostEstimate(
            flops=2 * TOK * width * depth, bytes_accessed=4 * 10**6, transcendentals=0
        ),
    )(ctx_own, share, got_share)
    if ring:
        got, keep_y, got_y, block_out = lax.optimization_barrier((got, keep_y, got_y, block_out))
        results = pl.pallas_call(
            step_kernel,
            out_shape=(jax.ShapeDtypeStruct((rows, width), F32),) * 4,
            in_specs=[SM] + [VM] * 7,
            out_specs=(VM,) * 4,
            compiler_params=SMALL,
        )(me, keep, keep_y, got, got_y, q_master, q_moment, q_second)
    else:
        results = adam(q_master, q_moment, q_second, summed)
    return (block_out, *results)


def solution(mesh):
    in_specs = (
        P(("dp", "rep"), None),
        P(("dp", "rep"), None),
        P(("dp", "rep"), None),
        P(("dp", "rep")),
        P("dp", None),
        P("dp", None),
        P("dp", None),
        P("dp", None),
        P("dp", None),
        P(None, "dp"),
    )
    out_specs = (P(("dp", "rep"), None), P("dp", None), P("dp", None), P("dp", None), P("dp", None))
    return jax.shard_map(
        functools.partial(per_device, mesh.shape["dp"] // CORES, mesh.shape["rep"]),
        mesh=mesh,
        in_specs=in_specs,
        out_specs=out_specs,
        check_vma=False,
    )
```

```python
import functools

import jax
import jax.numpy as jnp
from jax import lax
from jax.experimental import pallas as pl
from jax.experimental.pallas import tpu as pltpu
from jax.sharding import PartitionSpec as P

HEADS = 10
HEAD_DIM = 64
TOK = 448
CORES = 2
CORE_HEADS = HEADS // CORES
WIDE = CORE_HEADS * HEAD_DIM
CHAINS = 2
RING_MOST = 8

first_fix = 0.9999734386011124
second_fix = 0.8673804441052468
BF = jnp.bfloat16
F32 = jnp.float32
VM = pl.BlockSpec(memory_space=pltpu.VMEM)
SM = pl.BlockSpec(memory_space=pltpu.SMEM)
ANY = pl.BlockSpec(memory_space=pl.ANY)
LARGE = pltpu.CompilerParams(vmem_limit_bytes=56 * 2**20)
HBM = pl.BlockSpec(memory_space=pltpu.HBM)
SMALL = pltpu.CompilerParams(vmem_limit_bytes=4 * 2**20)


ROWS = ((1,), (1,))


def padded(width):
    return -(-width // 128) * 128


def dot(a, b, dims=((1,), (0,))):
    return lax.dot_general(a, b, (dims, ((), ())), preferred_element_type=F32)


def ring_order(chips):
    return list(range(0, chips, 2)) + list(range(chips - 1, 0, -2))


def ring_pairs(chips, step):
    order = ring_order(chips)
    return [
        (CORES * order[i] + c, CORES * order[(i + step) % chips] + c)
        for i in range(chips)
        for c in range(CORES)
    ]


def chip_at(me_ref, chips, step):
    chip = me_ref[0] // CORES
    odd = chip % 2
    place = (1 - odd) * (chip // 2) + odd * (chips - 1 - chip // 2)
    place = (place + step + chips) % chips
    back = (place >= chips // 2).astype(jnp.int32)
    return (1 - back) * (2 * place) + back * (2 * (chips - 1 - place) + 1)


def pack(parts, core):
    return jnp.concatenate([w[:, core * WIDE : (core + 1) * WIDE] for w in parts], axis=1)


def pack_kernel(me, q, k, v, o, keep, send, qv, kv, vv, ov, sem):
    moves = ((q, qv), (k, kv), (v, vv), (o, ov))
    copies = [pltpu.make_async_copy(src, dst, sem.at[i]) for i, (src, dst) in enumerate(moves)]
    for c in copies:
        c.start()
    for c in copies:
        c.wait()
    first = me[0] % CORES == 0
    parts = (qv[...].astype(BF), kv[...], vv[...], ov[...])
    halves = [pack(parts, c) for c in range(CORES)]

    @pl.when(first)
    def _():
        keep[...] = halves[0]
        send[...] = halves[1]

    @pl.when(jnp.logical_not(first))
    def _():
        keep[...] = halves[1]
        send[...] = halves[0]


def stage_kernel(length, x, e, g, _, acts, xv, ev, gv, sem):
    parts = list(zip((x, e, g), (xv, ev, gv), act_rows(e.shape[0])))
    loads = [pltpu.make_async_copy(a, v, sem.at[i]) for i, (a, v, _) in enumerate(parts)]
    stores = [pltpu.make_async_copy(v, acts.at[at], sem.at[3 + i]) for i, (_, v, at) in enumerate(parts)]
    for c in loads[::-1]:
        c.start()
    loads[2].wait()
    in_use = lax.broadcasted_iota(jnp.int32, gv.shape, 0) < length[0]
    gv[...] = jnp.where(in_use, gv[...].astype(F32), 0.0).astype(BF)
    stores[2].start()
    for i in (1, 0):
        loads[i].wait()
        stores[i].start()
    for c in stores:
        c.wait()


def act_rows(frames):
    return pl.ds(0, TOK), pl.ds(TOK, frames), pl.ds(TOK + frames, TOK)


def turn_kernel(mine, other, t0, t1):
    t0[...] = mine[:TOK, :].T
    t1[...] = other[:TOK, :].T


def turn(mine, other):
    return pl.pallas_call(
        turn_kernel,
        out_shape=(jax.ShapeDtypeStruct((mine.shape[1], TOK), BF),) * 2,
        in_specs=[VM] * 2,
        out_specs=(VM,) * 2,
        compiler_params=pltpu.CompilerParams(vmem_limit_bytes=8 * 2**20),
        cost_estimate=pl.CostEstimate(flops=0, bytes_accessed=5 * 10**6, transcendentals=0),
    )(mine, other)


def join_kernel(me, keep, got, *blocks):
    core = me[0] % CORES
    rows = keep.shape[0]
    mine = pl.ds(pl.multiple_of(core * rows, rows), rows)
    other = pl.ds(pl.multiple_of((1 - core) * rows, rows), rows)
    at = 0
    for block in blocks:
        cols = slice(at, at + block.shape[1])
        block[mine, :] = keep[:, cols]
        block[other, :] = got[:, cols]
        at += block.shape[1]


def head_kernel(chips, steps, pieces, *refs):
    refs = list(refs)
    take = lambda n: [refs.pop(0) for _ in range(n)]
    (me,) = take(1)
    chains = [take(len(s)) for s in steps]
    mine, other, t0, t1 = take(4)
    share, ctx_own = take(2)
    sums = take(len(pieces))
    w, whole = take(2)
    number, width = CORE_HEADS, WIDE
    chip_rows = w.shape[0] // chips
    if len(steps[0]) == 1:
        places = [0]
    else:
        places = [pl.multiple_of(chip_at(me, chips, k) * chip_rows, chip_rows) for k in range(chips)]
    cols = w.shape[1] // len(chains)
    for i, blocks in enumerate(chains):
        for k, block in zip(steps[i], blocks):
            w[pl.ds(places[k], block.shape[0]), i * cols : (i + 1) * cols] = block[...]

    _, e_at, g_at = act_rows(mine.shape[0] - 2 * TOK)
    rows_of = []

    wq_t, wo_t = w[:, :width].T, w[:, 3 * width :].T

    def project(clip):
        acts = (mine, other)[clip]
        qt = (dot(wq_t, (t0, t1)[clip][...]) * 0.125).astype(BF)
        kv = dot(acts[e_at, :], w[:, width : 3 * width]).astype(BF)
        gt = dot(wo_t, acts[g_at, :], ROWS).astype(BF)
        k, v = kv[:, :width], kv[:, width:]
        rows_of.append((qt, k, v, gt, k.T, v.T))

    def begin(clip, h, tokens):
        qt, k, v, gt, _, _ = rows_of[clip]
        cols = slice(h * HEAD_DIM, (h + 1) * HEAD_DIM)
        return dot(k[:, cols], qt[cols, tokens]), dot(v[:, cols], gt[cols, tokens])

    def finish(clip, h, tokens, scores, grad_attention):
        _, _, _, gt, kt, vt = rows_of[clip]
        cols = slice(h * HEAD_DIM, (h + 1) * HEAD_DIM)
        e = jnp.exp(scores - jnp.max(scores, axis=0, keepdims=True))
        attention = (e * (1.0 / jnp.sum(e, axis=0, keepdims=True))).astype(BF)
        ctx = dot(vt[cols], attention)
        inner = jnp.sum(gt[cols, tokens].astype(F32) * ctx, axis=0, keepdims=True)
        grad_scores = (attention.astype(F32) * (grad_attention - inner)).astype(BF)
        return ctx.astype(BF), (dot(kt[cols], grad_scores) * 0.125).astype(BF)

    halves = (slice(0, 256), slice(256, TOK))
    items = [(clip, h, t) for clip in range(2) for h in range(number) for t in halves]
    project(0)
    begun = [begin(*item) for item in items[:2]]
    done = []
    for i, item in enumerate(items):
        if i == 6:
            project(1)
        if i + 2 < len(items):
            begun.append(begin(*items[i + 2]))
        done.append(finish(*item, *begun[i]))
    ctxs, grads = [
        [
            jnp.concatenate(
                [
                    jnp.concatenate([done[(c * number + h) * 2 + t][which] for t in (0, 1)], axis=1)
                    for h in range(number)
                ],
                axis=0,
            ).T
            for c in (0, 1)
        ]
        for which in (0, 1)
    ]
    ctx_own[...] = ctxs[0]
    share[:TOK, :width] = ctxs[1]
    share[TOK:, :width] = w[:, 3 * width :]
    whole[...] = dot(t0[...], grads[0]) + dot(t1[...], grads[1])
    for out, (k, skip) in zip(sums, pieces):
        fold = out.shape[1] // width
        for i in range(fold):
            rows = pl.ds(places[k] + skip + i * out.shape[0], out.shape[0])
            out[:, i * width : (i + 1) * width] = whole[rows, :]


def heads(chips, me, chains, steps, acts, pieces, piece_shape):
    depth = acts[0].shape[1]
    width = WIDE
    blocks = [b for chain in chains for b in chain]
    return pl.pallas_call(
        functools.partial(head_kernel, chips, steps, pieces),
        out_shape=(
            jax.ShapeDtypeStruct((TOK + depth, padded(width)), BF),
            jax.ShapeDtypeStruct((TOK, width), BF),
        )
        + (jax.ShapeDtypeStruct(piece_shape, F32),) * len(pieces),
        in_specs=[SM] + [VM] * (len(blocks) + 4),
        out_specs=(VM,) * (2 + len(pieces)),
        scratch_shapes=[pltpu.VMEM((depth, 4 * width), BF)]
        + [pltpu.VMEM((depth, width), F32)],
        compiler_params=pltpu.CompilerParams(vmem_limit_bytes=22 * 2**20),
        cost_estimate=pl.CostEstimate(
            flops=9 * 10**9, bytes_accessed=15 * 10**6, transcendentals=2 * 10**6
        ),
    )(me, *blocks, *acts)


def out_kernel(ctx_own, share, got, out):
    out[...] = (
        dot(ctx_own[...], share[TOK:, :WIDE], ROWS) + dot(got[:TOK, :WIDE], got[TOK:, :WIDE], ROWS)
    ).astype(BF)


def total_kernel(me, *refs):
    *parts, keep, send = refs
    halves = [parts[i][...] + parts[i + 1][...] + parts[i + 2][...] for i in (0, 3)]
    for c in range(CORES):

        @pl.when(me[0] % CORES == c)
        def _():
            keep[...] = halves[c]
            send[...] = halves[1 - c]


def adam(q_master, q_moment, q_second, summed):
    q_gradient = summed * (1.0 / TOK)
    new_moment = 0.9 * q_moment + 0.1 * q_gradient
    new_second = 0.98 * q_second + 0.02 * q_gradient * q_gradient
    update = new_moment / first_fix / (jnp.sqrt(new_second / second_fix) + 1e-06)
    new_master = q_master - 0.001 * (update + 0.01 * q_master)
    return q_gradient, new_master, new_moment, new_second


def step_kernel(me, keep, keep_y, got, got_y, master, moment, second, *outs):
    core = me[0] % CORES
    mine = keep[...] + keep_y[...]
    other = got[...] + got_y[...]
    for c in range(CORES):

        @pl.when(core == c)
        def _():
            for i in range(2):
                rows = slice(i * mine.shape[0], (i + 1) * mine.shape[0])
                cols = slice(i * WIDE, (i + 1) * WIDE)
                halves = (mine[:, cols], other[:, cols])
                summed = jnp.concatenate([halves[c], halves[1 - c]], axis=1)
                values = adam(master[rows, :], moment[rows, :], second[rows, :], summed)
                for out, value in zip(outs, values):
                    out[rows, :] = value


def per_device(
    chips,
    reps,
    text_states,
    encoder_frames,
    out_cotangent,
    text_lengths,
    q_master,
    q_moment,
    q_second,
    key_weight,
    value_weight,
    out_weight,
):
    rows, width = q_master.shape
    frames, depth = encoder_frames.shape
    chip_rows = CORES * rows
    index = lax.axis_index("dp")
    me = index.astype(jnp.int32).reshape(1)
    first = index % CORES == 0
    mates = [(i, i ^ 1) for i in range(CORES * chips)]
    swap = lambda a: lax.ppermute(a, "dp", mates)
    ring = 1 < chips <= RING_MOST and reps == 2
    right = lambda a: lax.ppermute(a, "dp", ring_pairs(chips, 1))
    left = lambda a: lax.ppermute(a, "dp", ring_pairs(chips, -1))
    same_core = [[CORES * i + c for i in range(chips)] for c in range(CORES)]

    if ring:
        keep, send = pl.pallas_call(
            pack_kernel,
            out_shape=(jax.ShapeDtypeStruct((rows, 4 * WIDE), BF),) * 2,
            in_specs=[SM] + [HBM] * 4,
            out_specs=(VM,) * 2,
            scratch_shapes=[pltpu.VMEM((rows, width), F32)]
            + [pltpu.VMEM((rows, width), BF)] * 3
            + [pltpu.SemaphoreType.DMA((4,))],
            compiler_params=LARGE,
        )(me, q_master, key_weight, value_weight, out_weight.T)
        got = swap(send)
        mine = pl.pallas_call(
            stage_kernel,
            out_shape=jax.ShapeDtypeStruct((2 * TOK + frames, depth), BF),
            in_specs=[SM] + [HBM] * 3 + [ANY],
            out_specs=HBM,
            scratch_shapes=[pltpu.VMEM((n, depth), BF) for n in (TOK, frames, TOK)]
            + [pltpu.SemaphoreType.DMA((6,))],
            compiler_params=LARGE,
        )(text_lengths, text_states, encoder_frames, out_cotangent, keep)
        own_blocks = pl.pallas_call(
            join_kernel,
            out_shape=(jax.ShapeDtypeStruct((chip_rows, 4 * WIDE // CHAINS), BF),) * CHAINS,
            in_specs=[SM] + [VM] * 2,
            out_specs=(VM,) * CHAINS,
            compiler_params=SMALL,
        )(me, keep, got)
    else:
        parts = (q_master.astype(BF), key_weight, value_weight, out_weight.T)
        packs = [pack(parts, c) for c in range(CORES)]
        keep = jnp.where(first, packs[0], packs[1])
        got = swap(jnp.where(first, packs[1], packs[0]))
        block = jnp.where(
            first, jnp.concatenate([keep, got], axis=0), jnp.concatenate([got, keep], axis=0)
        )
        own_blocks = [block]
        in_use = jnp.arange(TOK, dtype=jnp.int32) < text_lengths[0]
        grad_out = jnp.where(in_use[:, None], out_cotangent, jnp.zeros_like(out_cotangent))
        mine = jnp.concatenate([text_states, encoder_frames, grad_out], axis=0)

    mine, *own_blocks = lax.optimization_barrier((mine, *own_blocks))
    other = swap(mine)
    acts = (mine, other, *turn(mine, other))
    far = chips // 2
    if ring:
        steps, chains = [], []
        for i, own in enumerate(own_blocks):
            at, blocks = [0], [own]
            r = l = own
            for k in range(1, far):
                r, l = right(r), left(l)
                at += [chips - k, k]
                blocks += [r, l]
            at += [far]
            blocks += [right(r) if i % 2 == 0 else left(l)]
            steps.append(at)
            chains.append(blocks)
        pieces = [(k, h * rows) for k in range(far, 0, -1) for h in range(2)]
        pieces += [(chips - k, h * rows) for k in range(far - 1, 0, -1) for h in range(2)]
        pieces += [(0, h * rows) for h in range(2)]
        share, ctx_own, *sums = heads(chips, me, chains, steps, acts, pieces, (rows // 2, 2 * WIDE))
        got_share = swap(share)
        totals = []
        for h in range(2):
            term = {k: s for (k, skip), s in zip(pieces, sums) if skip == h * rows}
            away, back, sign = (right, left, 1) if h == 0 else (left, right, -1)
            a, b = away(term[far]), back(term[-sign * (far - 1) % chips])
            for k in range(far - 1, 0, -1):
                a = away(a + term[sign * k % chips])
                if k > 1:
                    b = back(b + term[-sign * (k - 1) % chips])
            totals += [term[0], a, b]
        keep, send = pl.pallas_call(
            total_kernel,
            out_shape=(jax.ShapeDtypeStruct((rows // 2, 2 * WIDE), F32),) * 2,
            in_specs=[SM] + [VM] * len(totals),
            out_specs=(VM, VM),
            compiler_params=SMALL,
        )(me, *totals)
        both = ("dp", "rep")
        across = [(i * reps + y, i * reps + (1 - y)) for i in range(CORES * chips) for y in range(reps)]
        cross = [(i * reps + y, (i ^ 1) * reps + (1 - y)) for i in range(CORES * chips) for y in range(reps)]
        got = swap(send)
        keep_y = lax.ppermute(keep, both, across)
        got_y = lax.ppermute(send, both, cross)
    else:
        block = lax.all_gather(own_blocks[0], "dp", axis=0, tiled=True, axis_index_groups=same_core)
        share, ctx_own, total = heads(chips, me, [[block]], [[0]], acts, [(0, 0)], (depth, WIDE))
        got_share = swap(share)
        total = lax.psum_scatter(
            total, "dp", scatter_dimension=0, tiled=True, axis_index_groups=same_core
        )
        keep = jnp.where(first, total[:rows], total[rows:])
        got = swap(jnp.where(first, total[rows:], total[:rows]))
        summed = jnp.where(
            first, jnp.concatenate([keep, got], axis=1), jnp.concatenate([got, keep], axis=1)
        )
        summed = lax.psum(summed, "rep")

    block_out = pl.pallas_call(
        out_kernel,
        out_shape=jax.ShapeDtypeStruct((TOK, depth), BF),
        in_specs=[VM] * 3,
        out_specs=VM,
        compiler_params=pltpu.CompilerParams(vmem_limit_bytes=8 * 2**20),
        cost_estimate=pl.CostEstimate(
            flops=2 * TOK * width * depth, bytes_accessed=4 * 10**6, transcendentals=0
        ),
    )(ctx_own, share, got_share)
    if ring:
        got, keep_y, got_y, block_out = lax.optimization_barrier((got, keep_y, got_y, block_out))
        results = pl.pallas_call(
            step_kernel,
            out_shape=(jax.ShapeDtypeStruct((rows, width), F32),) * 4,
            in_specs=[SM] + [VM] * 7,
            out_specs=(VM,) * 4,
            compiler_params=SMALL,
        )(me, keep, keep_y, got, got_y, q_master, q_moment, q_second)
    else:
        results = adam(q_master, q_moment, q_second, summed)
    return (block_out, *results)


def solution(mesh):
    in_specs = (
        P(("dp", "rep"), None),
        P(("dp", "rep"), None),
        P(("dp", "rep"), None),
        P(("dp", "rep")),
        P("dp", None),
        P("dp", None),
        P("dp", None),
        P("dp", None),
        P("dp", None),
        P(None, "dp"),
    )
    out_specs = (P(("dp", "rep"), None), P("dp", None), P("dp", None), P("dp", None), P("dp", None))
    return jax.shard_map(
        functools.partial(per_device, mesh.shape["dp"] // CORES, mesh.shape["rep"]),
        mesh=mesh,
        in_specs=in_specs,
        out_specs=out_specs,
        check_vma=False,
    )
```

```python
import functools

import jax
import jax.numpy as jnp
from jax import lax
from jax.experimental import pallas as pl
from jax.experimental.pallas import tpu as pltpu
from jax.sharding import PartitionSpec as P

HEADS = 10
HEAD_DIM = 64
TOK = 448
CORES = 2
CORE_HEADS = HEADS // CORES
WIDE = CORE_HEADS * HEAD_DIM
CHAINS = 2
RING_MOST = 8

first_fix = 0.9999734386011124
second_fix = 0.8673804441052468
BF = jnp.bfloat16
F32 = jnp.float32
VM = pl.BlockSpec(memory_space=pltpu.VMEM)
SM = pl.BlockSpec(memory_space=pltpu.SMEM)
ANY = pl.BlockSpec(memory_space=pl.ANY)
LARGE = pltpu.CompilerParams(vmem_limit_bytes=56 * 2**20)
HBM = pl.BlockSpec(memory_space=pltpu.HBM)
SMALL = pltpu.CompilerParams(vmem_limit_bytes=4 * 2**20)


ROWS = ((1,), (1,))


def padded(width):
    return -(-width // 128) * 128


def dot(a, b, dims=((1,), (0,))):
    return lax.dot_general(a, b, (dims, ((), ())), preferred_element_type=F32)


def ring_order(chips):
    return list(range(0, chips, 2)) + list(range(chips - 1, 0, -2))


def ring_pairs(chips, step):
    order = ring_order(chips)
    return [
        (CORES * order[i] + c, CORES * order[(i + step) % chips] + c)
        for i in range(chips)
        for c in range(CORES)
    ]


def chip_at(me_ref, chips, step):
    chip = me_ref[0] // CORES
    odd = chip % 2
    place = (1 - odd) * (chip // 2) + odd * (chips - 1 - chip // 2)
    place = (place + step + chips) % chips
    back = (place >= chips // 2).astype(jnp.int32)
    return (1 - back) * (2 * place) + back * (2 * (chips - 1 - place) + 1)


def pack(parts, core):
    return jnp.concatenate([w[:, core * WIDE : (core + 1) * WIDE] for w in parts], axis=1)


def pack_kernel(me, q, k, v, o, keep, send, qv, kv, vv, ov, sem):
    moves = ((q, qv), (k, kv), (v, vv), (o, ov))
    copies = [pltpu.make_async_copy(src, dst, sem.at[i]) for i, (src, dst) in enumerate(moves)]
    for c in copies:
        c.start()
    for c in copies:
        c.wait()
    first = me[0] % CORES == 0
    parts = (qv[...].astype(BF), kv[...], vv[...], ov[...])
    halves = [pack(parts, c) for c in range(CORES)]

    @pl.when(first)
    def _():
        keep[...] = halves[0]
        send[...] = halves[1]

    @pl.when(jnp.logical_not(first))
    def _():
        keep[...] = halves[1]
        send[...] = halves[0]


def stage_kernel(length, x, e, g, _, acts, xv, ev, gv, sem):
    parts = list(zip((x, e, g), (xv, ev, gv), act_rows(e.shape[0])))
    loads = [pltpu.make_async_copy(a, v, sem.at[i]) for i, (a, v, _) in enumerate(parts)]
    stores = [pltpu.make_async_copy(v, acts.at[at], sem.at[3 + i]) for i, (_, v, at) in enumerate(parts)]
    for c in loads[::-1]:
        c.start()
    loads[2].wait()
    in_use = lax.broadcasted_iota(jnp.int32, gv.shape, 0) < length[0]
    gv[...] = jnp.where(in_use, gv[...], jnp.zeros_like(gv))
    stores[2].start()
    for i in (1, 0):
        loads[i].wait()
        stores[i].start()
    for c in stores:
        c.wait()


def act_rows(frames):
    return pl.ds(0, TOK), pl.ds(TOK, frames), pl.ds(TOK + frames, TOK)


def turn_kernel(mine, other, t0, t1):
    t0[...] = mine[:TOK, :].T
    t1[...] = other[:TOK, :].T


def turn(mine, other):
    return pl.pallas_call(
        turn_kernel,
        out_shape=(jax.ShapeDtypeStruct((mine.shape[1], TOK), BF),) * 2,
        in_specs=[VM] * 2,
        out_specs=(VM,) * 2,
        compiler_params=pltpu.CompilerParams(vmem_limit_bytes=8 * 2**20),
        cost_estimate=pl.CostEstimate(flops=0, bytes_accessed=5 * 10**6, transcendentals=0),
    )(mine, other)


def join_kernel(me, keep, got, *blocks):
    core = me[0] % CORES
    rows = keep.shape[0]
    mine = pl.ds(pl.multiple_of(core * rows, rows), rows)
    other = pl.ds(pl.multiple_of((1 - core) * rows, rows), rows)
    at = 0
    for block in blocks:
        cols = slice(at, at + block.shape[1])
        block[mine, :] = keep[:, cols]
        block[other, :] = got[:, cols]
        at += block.shape[1]


def head_kernel(chips, steps, pieces, *refs):
    refs = list(refs)
    take = lambda n: [refs.pop(0) for _ in range(n)]
    (me,) = take(1)
    chains = [take(len(s)) for s in steps]
    mine, other, t0, t1 = take(4)
    share, ctx_own = take(2)
    sums = take(len(pieces))
    w, whole = take(2)
    number, width = CORE_HEADS, WIDE
    chip_rows = w.shape[0] // chips
    if len(steps[0]) == 1:
        places = [0]
    else:
        places = [pl.multiple_of(chip_at(me, chips, k) * chip_rows, chip_rows) for k in range(chips)]
    cols = w.shape[1] // len(chains)
    for i, blocks in enumerate(chains):
        for k, block in zip(steps[i], blocks):
            w[pl.ds(places[k], block.shape[0]), i * cols : (i + 1) * cols] = block[...]

    _, e_at, g_at = act_rows(mine.shape[0] - 2 * TOK)
    rows_of = []

    wq_t, wo_t = w[:, :width].T, w[:, 3 * width :].T

    def project(clip):
        acts = (mine, other)[clip]
        qt = (dot(wq_t, (t0, t1)[clip][...]) * 0.125).astype(BF)
        kv = dot(acts[e_at, :], w[:, width : 3 * width]).astype(BF)
        gt = dot(wo_t, acts[g_at, :], ROWS).astype(BF)
        k, v = kv[:, :width], kv[:, width:]
        rows_of.append((qt, k, v, gt, k.T, v.T))

    def begin(clip, h, tokens):
        qt, k, v, gt, _, _ = rows_of[clip]
        cols = slice(h * HEAD_DIM, (h + 1) * HEAD_DIM)
        return dot(k[:, cols], qt[cols, tokens]), dot(v[:, cols], gt[cols, tokens])

    def finish(clip, h, tokens, scores, grad_attention):
        _, _, _, gt, kt, vt = rows_of[clip]
        cols = slice(h * HEAD_DIM, (h + 1) * HEAD_DIM)
        e = jnp.exp(scores - jnp.max(scores, axis=0, keepdims=True))
        attention = (e * (1.0 / jnp.sum(e, axis=0, keepdims=True))).astype(BF)
        ctx = dot(vt[cols], attention)
        inner = jnp.sum(gt[cols, tokens].astype(F32) * ctx, axis=0, keepdims=True)
        grad_scores = (attention.astype(F32) * (grad_attention - inner)).astype(BF)
        return ctx.astype(BF), (dot(kt[cols], grad_scores) * 0.125).astype(BF)

    halves = (slice(0, 256), slice(256, TOK))
    items = [(clip, h, t) for clip in range(2) for h in range(number) for t in halves]
    project(0)
    begun = [begin(*item) for item in items[:3]]
    done = []
    for i, item in enumerate(items):
        if i == 6:
            project(1)
        if i + 3 < len(items):
            begun.append(begin(*items[i + 3]))
        done.append(finish(*item, *begun[i]))
    ctxs, grads = [
        [
            jnp.concatenate(
                [
                    jnp.concatenate([done[(c * number + h) * 2 + t][which] for t in (0, 1)], axis=1)
                    for h in range(number)
                ],
                axis=0,
            ).T
            for c in (0, 1)
        ]
        for which in (0, 1)
    ]
    ctx_own[...] = ctxs[0]
    share[:TOK, :width] = ctxs[1]
    share[TOK:, :width] = w[:, 3 * width :]
    whole[...] = dot(t0[...], grads[0]) + dot(t1[...], grads[1])
    for out, (k, skip) in zip(sums, pieces):
        fold = out.shape[1] // width
        for i in range(fold):
            rows = pl.ds(places[k] + skip + i * out.shape[0], out.shape[0])
            out[:, i * width : (i + 1) * width] = whole[rows, :]


def heads(chips, me, chains, steps, acts, pieces, piece_shape):
    depth = acts[0].shape[1]
    width = WIDE
    blocks = [b for chain in chains for b in chain]
    return pl.pallas_call(
        functools.partial(head_kernel, chips, steps, pieces),
        out_shape=(
            jax.ShapeDtypeStruct((TOK + depth, padded(width)), BF),
            jax.ShapeDtypeStruct((TOK, width), BF),
        )
        + (jax.ShapeDtypeStruct(piece_shape, F32),) * len(pieces),
        in_specs=[SM] + [VM] * (len(blocks) + 4),
        out_specs=(VM,) * (2 + len(pieces)),
        scratch_shapes=[pltpu.VMEM((depth, 4 * width), BF)]
        + [pltpu.VMEM((depth, width), F32)],
        compiler_params=pltpu.CompilerParams(vmem_limit_bytes=22 * 2**20),
        cost_estimate=pl.CostEstimate(
            flops=9 * 10**9, bytes_accessed=15 * 10**6, transcendentals=2 * 10**6
        ),
    )(me, *blocks, *acts)


def out_kernel(ctx_own, share, got, out):
    out[...] = (
        dot(ctx_own[...], share[TOK:, :WIDE], ROWS) + dot(got[:TOK, :WIDE], got[TOK:, :WIDE], ROWS)
    ).astype(BF)


def total_kernel(me, *refs):
    *parts, keep, send = refs
    halves = [parts[i][...] + parts[i + 1][...] + parts[i + 2][...] for i in (0, 3)]
    for c in range(CORES):

        @pl.when(me[0] % CORES == c)
        def _():
            keep[...] = halves[c]
            send[...] = halves[1 - c]


def adam(q_master, q_moment, q_second, summed):
    q_gradient = summed * (1.0 / TOK)
    new_moment = 0.9 * q_moment + 0.1 * q_gradient
    new_second = 0.98 * q_second + 0.02 * q_gradient * q_gradient
    update = new_moment / first_fix / (jnp.sqrt(new_second / second_fix) + 1e-06)
    new_master = q_master - 0.001 * (update + 0.01 * q_master)
    return q_gradient, new_master, new_moment, new_second


def step_kernel(me, keep, keep_y, got, got_y, master, moment, second, *outs):
    core = me[0] % CORES
    mine = keep[...] + keep_y[...]
    other = got[...] + got_y[...]
    for c in range(CORES):

        @pl.when(core == c)
        def _():
            for i in range(2):
                rows = slice(i * mine.shape[0], (i + 1) * mine.shape[0])
                cols = slice(i * WIDE, (i + 1) * WIDE)
                halves = (mine[:, cols], other[:, cols])
                summed = jnp.concatenate([halves[c], halves[1 - c]], axis=1)
                values = adam(master[rows, :], moment[rows, :], second[rows, :], summed)
                for out, value in zip(outs, values):
                    out[rows, :] = value


def per_device(
    chips,
    reps,
    text_states,
    encoder_frames,
    out_cotangent,
    text_lengths,
    q_master,
    q_moment,
    q_second,
    key_weight,
    value_weight,
    out_weight,
):
    rows, width = q_master.shape
    frames, depth = encoder_frames.shape
    chip_rows = CORES * rows
    index = lax.axis_index("dp")
    me = index.astype(jnp.int32).reshape(1)
    first = index % CORES == 0
    mates = [(i, i ^ 1) for i in range(CORES * chips)]
    swap = lambda a: lax.ppermute(a, "dp", mates)
    ring = 1 < chips <= RING_MOST and reps == 2
    right = lambda a: lax.ppermute(a, "dp", ring_pairs(chips, 1))
    left = lambda a: lax.ppermute(a, "dp", ring_pairs(chips, -1))
    same_core = [[CORES * i + c for i in range(chips)] for c in range(CORES)]

    if ring:
        keep, send = pl.pallas_call(
            pack_kernel,
            out_shape=(jax.ShapeDtypeStruct((rows, 4 * WIDE), BF),) * 2,
            in_specs=[SM] + [HBM] * 4,
            out_specs=(VM,) * 2,
            scratch_shapes=[pltpu.VMEM((rows, width), F32)]
            + [pltpu.VMEM((rows, width), BF)] * 3
            + [pltpu.SemaphoreType.DMA((4,))],
            compiler_params=LARGE,
        )(me, q_master, key_weight, value_weight, out_weight.T)
        got = swap(send)
        mine = pl.pallas_call(
            stage_kernel,
            out_shape=jax.ShapeDtypeStruct((2 * TOK + frames, depth), BF),
            in_specs=[SM] + [HBM] * 3 + [ANY],
            out_specs=HBM,
            scratch_shapes=[pltpu.VMEM((n, depth), BF) for n in (TOK, frames, TOK)]
            + [pltpu.SemaphoreType.DMA((6,))],
            compiler_params=LARGE,
        )(text_lengths, text_states, encoder_frames, out_cotangent, keep)
        own_blocks = pl.pallas_call(
            join_kernel,
            out_shape=(jax.ShapeDtypeStruct((chip_rows, 4 * WIDE // CHAINS), BF),) * CHAINS,
            in_specs=[SM] + [VM] * 2,
            out_specs=(VM,) * CHAINS,
            compiler_params=SMALL,
        )(me, keep, got)
    else:
        parts = (q_master.astype(BF), key_weight, value_weight, out_weight.T)
        packs = [pack(parts, c) for c in range(CORES)]
        keep = jnp.where(first, packs[0], packs[1])
        got = swap(jnp.where(first, packs[1], packs[0]))
        block = jnp.where(
            first, jnp.concatenate([keep, got], axis=0), jnp.concatenate([got, keep], axis=0)
        )
        own_blocks = [block]
        in_use = jnp.arange(TOK, dtype=jnp.int32) < text_lengths[0]
        grad_out = jnp.where(in_use[:, None], out_cotangent, jnp.zeros_like(out_cotangent))
        mine = jnp.concatenate([text_states, encoder_frames, grad_out], axis=0)

    mine, *own_blocks = lax.optimization_barrier((mine, *own_blocks))
    other = swap(mine)
    acts = (mine, other, *turn(mine, other))
    far = chips // 2
    if ring:
        steps, chains = [], []
        for i, own in enumerate(own_blocks):
            at, blocks = [0], [own]
            r = l = own
            for k in range(1, far):
                r, l = right(r), left(l)
                at += [chips - k, k]
                blocks += [r, l]
            at += [far]
            blocks += [right(r) if i % 2 == 0 else left(l)]
            steps.append(at)
            chains.append(blocks)
        pieces = [(k, h * rows) for k in range(far, 0, -1) for h in range(2)]
        pieces += [(chips - k, h * rows) for k in range(far - 1, 0, -1) for h in range(2)]
        pieces += [(0, h * rows) for h in range(2)]
        share, ctx_own, *sums = heads(chips, me, chains, steps, acts, pieces, (rows // 2, 2 * WIDE))
        got_share = swap(share)
        totals = []
        for h in range(2):
            term = {k: s for (k, skip), s in zip(pieces, sums) if skip == h * rows}
            away, back, sign = (right, left, 1) if h == 0 else (left, right, -1)
            a, b = away(term[far]), back(term[-sign * (far - 1) % chips])
            for k in range(far - 1, 0, -1):
                a = away(a + term[sign * k % chips])
                if k > 1:
                    b = back(b + term[-sign * (k - 1) % chips])
            totals += [term[0], a, b]
        keep, send = pl.pallas_call(
            total_kernel,
            out_shape=(jax.ShapeDtypeStruct((rows // 2, 2 * WIDE), F32),) * 2,
            in_specs=[SM] + [VM] * len(totals),
            out_specs=(VM, VM),
            compiler_params=SMALL,
        )(me, *totals)
        both = ("dp", "rep")
        across = [(i * reps + y, i * reps + (1 - y)) for i in range(CORES * chips) for y in range(reps)]
        cross = [(i * reps + y, (i ^ 1) * reps + (1 - y)) for i in range(CORES * chips) for y in range(reps)]
        got = swap(send)
        keep_y = lax.ppermute(keep, both, across)
        got_y = lax.ppermute(send, both, cross)
    else:
        block = lax.all_gather(own_blocks[0], "dp", axis=0, tiled=True, axis_index_groups=same_core)
        share, ctx_own, total = heads(chips, me, [[block]], [[0]], acts, [(0, 0)], (depth, WIDE))
        got_share = swap(share)
        total = lax.psum_scatter(
            total, "dp", scatter_dimension=0, tiled=True, axis_index_groups=same_core
        )
        keep = jnp.where(first, total[:rows], total[rows:])
        got = swap(jnp.where(first, total[rows:], total[:rows]))
        summed = jnp.where(
            first, jnp.concatenate([keep, got], axis=1), jnp.concatenate([got, keep], axis=1)
        )
        summed = lax.psum(summed, "rep")

    block_out = pl.pallas_call(
        out_kernel,
        out_shape=jax.ShapeDtypeStruct((TOK, depth), BF),
        in_specs=[VM] * 3,
        out_specs=VM,
        compiler_params=pltpu.CompilerParams(vmem_limit_bytes=8 * 2**20),
        cost_estimate=pl.CostEstimate(
            flops=2 * TOK * width * depth, bytes_accessed=4 * 10**6, transcendentals=0
        ),
    )(ctx_own, share, got_share)
    if ring:
        got, keep_y, got_y, block_out = lax.optimization_barrier((got, keep_y, got_y, block_out))
        results = pl.pallas_call(
            step_kernel,
            out_shape=(jax.ShapeDtypeStruct((rows, width), F32),) * 4,
            in_specs=[SM] + [VM] * 7,
            out_specs=(VM,) * 4,
            compiler_params=SMALL,
        )(me, keep, keep_y, got, got_y, q_master, q_moment, q_second)
    else:
        results = adam(q_master, q_moment, q_second, summed)
    return (block_out, *results)


def solution(mesh):
    in_specs = (
        P(("dp", "rep"), None),
        P(("dp", "rep"), None),
        P(("dp", "rep"), None),
        P(("dp", "rep")),
        P("dp", None),
        P("dp", None),
        P("dp", None),
        P("dp", None),
        P("dp", None),
        P(None, "dp"),
    )
    out_specs = (P(("dp", "rep"), None), P("dp", None), P("dp", None), P("dp", None), P("dp", None))
    return jax.shard_map(
        functools.partial(per_device, mesh.shape["dp"] // CORES, mesh.shape["rep"]),
        mesh=mesh,
        in_specs=in_specs,
        out_specs=out_specs,
        check_vma=False,
    )
```
